256 devices in a mesh: seq: 64 (over y, z_hi, x), head: 4 (over z_lo, core).
Axes of the slice: x: 4, y: 4, z: 8 (z_hi: 4, z_lo: 2; z = z_hi * 2 + z_lo), core: 2. Of those that a mesh axis runs over, the one named last changes fastest.
Arguments:
- tokens: bfloat16 [16384, 1536], P('seq'), may hold values from -200 to 200
- query_weight: bfloat16 [1536, 1536], P(None, 'head'), may hold values from -0.15625 to 0.15625
- key_weight: bfloat16 [1536, 1536], P(None, 'head'), may hold values from -0.15625 to 0.15625
- value_weight: bfloat16 [1536, 1536], P(None, 'head'), may hold values from -0.15625 to 0.15625
- offsets: int32 [4, 24], P(None, 'head'), may hold values from 0 to 7
- out_weight: bfloat16 [1536, 1536], P('head'), may hold values from -0.15625 to 0.15625
Outputs:
- layer_out: bfloat16 [16384, 1536], P(('seq', 'head'))
The draws below stay inside these ranges and needn't reach their ends.
All inputs are finite; a program needn't handle non-finite values.
Results may differ from the reference program's by a relative error of at most 0.0095.
The reference program's roundings to bfloat16 on the way (of `attention`) count: a program that leaves them out, or rounds other values in their place, can miss the bound.
Values may be sent and summed in bfloat16 or wider, within the bound.
A program may use at most 64 MiB of HBM per device.

```python
import jax
import jax.numpy as jnp
from jax import lax

D = 1536
HEADS = 24
HDIM = 64
LEVELS = 4
SEQ = 16384
SPAN = 2048


def draw_tokens(key, part):
    key = jax.random.fold_in(key, 11)
    base_key = jax.random.fold_in(key, 0)
    base = jnp.clip(jax.random.normal(base_key, (SEQ, D), jnp.float32), -6.0, 6.0)
    return base.astype(jnp.bfloat16)


def with_ends(result, own_key, smallest, high):
    index_at = [jax.random.randint(jax.random.fold_in(own_key, axis), (), 0, length) for axis, length in enumerate(result.shape)]
    longest = result.shape.index(max(result.shape))
    next_to = index_at[:longest] + [(index_at[longest] + 1) % result.shape[longest]] + index_at[longest + 1:]
    return result.at[tuple(index_at)].set(smallest).at[tuple(next_to)].set(high)


def block_scale(stream_key, extent, cuts, least, largest):
    def one(position, parts):
        heights = jax.random.uniform(jax.random.fold_in(jax.random.fold_in(stream_key, 6), position), (parts,), jnp.float32, least / len(cuts), largest / len(cuts))
        return jnp.repeat(jnp.exp(heights), extent[position] // parts).reshape((-1,) + (1,) * (len(extent) - position - 1))

    factor_of = one(*cuts[0])
    for cut in cuts[1:]:
        factor_of = factor_of * one(*cut)
    return factor_of


def noise(rng, shape, spread, most, shards=(), held_as=jnp.bfloat16):
    entries = spread * jax.random.normal(rng, shape, jnp.float32)
    if shards:
        entries = entries * block_scale(rng, shape, shards, -0.22, 0.18)
    return jnp.clip(entries, -most, most).astype(held_as)


def setup_inputs(seed: int = 0) -> dict:
    arg_keys = jax.random.split(jax.random.key(seed), 7)
    return {
        "tokens": draw_tokens(jax.random.fold_in(arg_keys[6], 71), 0),
        "query_weight": noise(arg_keys[1], (D, D), D ** -0.5, 0.15625, ((1, 4),)),
        "key_weight": noise(arg_keys[2], (D, D), D ** -0.5, 0.15625, ((1, 4),)),
        "value_weight": noise(arg_keys[3], (D, D), D ** -0.5, 0.15625, ((1, 4),)),
        "offsets": with_ends(jax.random.randint(arg_keys[4], (LEVELS, HEADS), 0, 8), jax.random.fold_in(arg_keys[4], 1), 0, 7).astype(jnp.int32),
        "out_weight": noise(arg_keys[5], (D, D), D ** -0.5, 0.15625, ((0, 4),)),
    }


score_scale = 0.125
absent_value = -1.0e30


def select(values, stride, offset):
    shaped = values.reshape(values.shape[0] // stride, stride, values.shape[1], values.shape[2])
    picker = (jnp.arange(stride, dtype=jnp.int32)[:, None] == offset[None, :]).astype(values.dtype)
    return jnp.sum(shaped * picker[None, :, :, None], axis=1).astype(values.dtype)


def attend(triple):
    query_set, key_set, value_set = triple
    scores = jnp.dot(query_set, key_set.T, preferred_element_type=jnp.float32) * score_scale
    row_max = jnp.max(scores, axis=1)
    probs = jnp.exp(scores - row_max[:, None])
    total = jnp.sum(probs, axis=1)
    mixed = jnp.dot(probs.astype(jnp.bfloat16), value_set, preferred_element_type=jnp.float32) / total[:, None]
    return mixed, row_max + jnp.log(total)


def reference(tokens, query_weight, key_weight, value_weight, offsets, out_weight):
    def project(weight):
        return jnp.dot(tokens, weight, preferred_element_type=jnp.float32).astype(jnp.bfloat16).reshape(SEQ, HEADS, HDIM)

    queries = project(query_weight)
    key_rows = project(key_weight)
    value_rows = project(value_weight)
    mixed_all = []
    log_all = []
    for level_no in range(LEVELS):
        stride = 2 ** level_no
        segment_count = SEQ // (SPAN * stride)
        offset = (offsets[level_no] % stride).astype(jnp.int32)

        def arrange(values):
            picked = select(values, stride, offset).reshape(segment_count, SPAN, HEADS, HDIM)
            return picked.transpose(2, 0, 1, 3).reshape(HEADS * segment_count, SPAN, HDIM)

        mixed, log_total = lax.map(attend, (arrange(queries), arrange(key_rows), arrange(value_rows)))
        mixed = mixed.reshape(HEADS, segment_count, SPAN, HDIM).transpose(1, 2, 0, 3).reshape(SEQ // stride, HEADS, HDIM)
        log_total = log_total.reshape(HEADS, segment_count, SPAN).transpose(1, 2, 0).reshape(SEQ // stride, HEADS)
        picker = jnp.arange(stride, dtype=jnp.int32)[:, None] == offset[None, :]
        full_mixed = mixed[:, None, :, :] * picker[None, :, :, None].astype(jnp.float32)
        full_log = jnp.where(picker[None, :, :], log_total[:, None, :], jnp.float32(absent_value))
        mixed_all.append(full_mixed.reshape(SEQ, HEADS, HDIM))
        log_all.append(full_log.reshape(SEQ, HEADS))
    stacked_log = jnp.stack(log_all)
    best = jnp.max(stacked_log, axis=0)
    weights = jnp.exp(stacked_log - best[None])
    weight_sum = jnp.sum(weights, axis=0)
    combined = sum(weights[level_no][:, :, None] * mixed_all[level_no] for level_no in range(LEVELS))
    attention = (combined / weight_sum[:, :, None]).astype(jnp.bfloat16).reshape(SEQ, D)
    return jnp.dot(attention, out_weight, preferred_element_type=jnp.float32).astype(jnp.bfloat16)
```

```python
import jax
import jax.numpy as jnp
from jax import lax
from jax.experimental import pallas as pl
from jax.experimental.pallas import tpu as pltpu
from jax.sharding import PartitionSpec as P

MESH = pl.DeviceIdType.MESH
BF = jnp.bfloat16
F32 = jnp.float32
ROWS = 256
D = 1536
HALF = 128
CH = 64
SCALE = 0.125
LOG2E = 1.4426950408889634
ABSENT = -1e30


def nt(a, b):
    return lax.dot_general(a, b, (((1,), (1,)), ((), ())), preferred_element_type=F32)


def mm(a, b):
    return jnp.dot(a, b, preferred_element_type=F32)


def body(
    tok, w, wout, offs, out,
    T, KV, QQ, ZKV1, ZKV2, ZKV3, ZQ, PQ0, PQ1F, PQ1H, PQ2, PQ3,
    KA, QA, KB, QB, VX, RA, RB, R0, R123, ATT, ATTP, SB1, RB1, SB2, RB2, ACC,
    ts, tr, cs, cr, ls, lr, rs, rr0, rr, ps, pr, s1, r1, s2, r2, loc,
):
    sq = lax.axis_index("seq")
    hd = lax.axis_index("head")
    y = sq // 16
    zh = (sq // 4) % 4
    x = sq % 4
    zl = hd // 2
    core = hd % 2
    par = zh % 2
    p = zh // 2
    fi = 2 * p

    def seq_at(yy, zz, xx):
        return yy * 16 + zz * 4 + xx

    dz = 2 * zl - 1
    g_out = (zh + dz + 4) % 4
    n_out = (seq_at(y, g_out, x), (1 - zl) * 2 + core)
    n_in = (sq, (1 - zl) * 2 + core)
    n_core = (sq, zl * 2 + (1 - core))

    def rcopy(src, dst, ssem, rsem, dev):
        return pltpu.make_async_remote_copy(
            src_ref=src, dst_ref=dst, send_sem=ssem, recv_sem=rsem, device_id=dev, device_id_type=MESH
        )

    def send(src, dst, ssem, rsem, dst_seq):
        @pl.when(dst_seq != sq)
        def _():
            rcopy(src, dst, ssem, rsem, (dst_seq, hd)).start()

        @pl.when(dst_seq == sq)
        def _():
            pltpu.make_async_copy(src, dst, rsem).start()

    def sent(src, dst, ssem, rsem, dst_seq):
        @pl.when(dst_seq != sq)
        def _():
            rcopy(src, dst, ssem, rsem, (dst_seq, hd)).wait_send()

    def arrived(ref, sem):
        pltpu.make_async_copy(ref, ref, sem).wait()

    lo = core * HALF

    def rows_of(sub):
        return pl.ds(pl.multiple_of(lo + sub * CH, CH), CH)

    first, second = 1 - zl, zl
    own_sends = []
    for n, sub in enumerate((first, second)):
        c = rcopy(tok.at[rows_of(sub)], T.at[0, rows_of(sub)], ts.at[n], tr.at[n], n_out)
        c.start()
        own_sends.append(c)

    lane = lax.broadcasted_iota(jnp.int32, (1, 128), 1)
    low = lane < 64

    def targets(h, i):
        o1 = offs[1, 3 * par + h] & 1
        o2 = offs[2, 3 * par + h] & 3
        o3 = offs[3, 3 * par + h] & 7
        t1 = i * 2 + o1
        t2 = (i - 128) * 4 + o2
        t3 = (i - 192) * 8 + o3
        return jnp.where(i < 128, t1, jnp.where(i < 192, t2, jnp.where(i < 224, t3, -1)))

    def sel(h):
        i = lax.broadcasted_iota(jnp.int32, (ROWS, ROWS), 0)
        c = lax.broadcasted_iota(jnp.int32, (ROWS, ROWS), 1)
        return jnp.where(targets(h, i) == c, 1.0, 0.0).astype(BF)

    def sel_t(h, first_row, last_row):
        i = lax.broadcasted_iota(jnp.int32, (ROWS, ROWS), 1)
        c = lax.broadcasted_iota(jnp.int32, (ROWS, ROWS), 0)
        hit = (targets(h, i) == c) & (i >= first_row) & (i < last_row)
        return jnp.where(hit, 1.0, 0.0).astype(BF)

    def role_seq(role, yy):
        return seq_at(yy, zh, (role + 2 * core) % 4)

    x_of = (x + 2 * core) % 4

    def l0_kv(slot_blk, h):
        src = KV.at[slot_blk, h]
        dst = KA.at[pl.ds(pl.multiple_of(x * 512 + (slot_blk % 2) * 256, 256), 256)]
        return src, dst, ls.at[h, slot_blk % 2], lr.at[0], role_seq(h, y)

    def l0_q(h):
        dst = QA.at[pl.ds(pl.multiple_of(x * 256, 256), 256)]
        return PQ0.at[h], dst, ls.at[h, 2], lr.at[1], role_seq(h, y)

    def l1_kv(blk, j):
        dst_ref = (KA, KB)[j]
        dst = dst_ref.at[pl.ds(pl.multiple_of(x * 512 + blk * 128, 128), 128)]
        return ZKV1.at[j, blk], dst, ls.at[3 + j, blk], lr.at[2 * j], role_seq(3, y)

    def l1_q(j):
        if j == 0:
            return PQ1F, QA.at[pl.ds(pl.multiple_of(x * 256, 256), 256)], ls.at[5, 0], lr.at[1], role_seq(3, y)
        return PQ1H, QB.at[pl.ds(pl.multiple_of(x * 128, 128), 128)], ls.at[5, 1], lr.at[3], role_seq(3, y)

    def l2_kv(j):
        si = (y % 2) * 4 + x
        dst = KB.at[pl.ds(pl.multiple_of(si * 256, 256), 256)]
        return ZKV2.at[j // 2], dst, ls.at[6, j], lr.at[2], role_seq(j, y - y % 2)

    def l2_q(j):
        si = (y % 2) * 4 + x
        dst = QB.at[pl.ds(pl.multiple_of(si * 64, 64), 64)]
        return PQ2.at[j], dst, ls.at[7, j], lr.at[3], role_seq(j, y - y % 2)

    def l3_kv(j):
        si = y * 4 + x
        dst = KB.at[pl.ds(pl.multiple_of(si * 128, 128), 128)]
        return ZKV3.at[j // 2], dst, ls.at[8, j], lr.at[2], role_seq(j, 1)

    def l3_q(j):
        si = y * 4 + x
        dst = QB.at[pl.ds(pl.multiple_of(si * 32, 32), 32)]
        return PQ3.at[j], dst, ls.at[9, j], lr.at[3], role_seq(j, 1)

    def project(x_ref, blk):
        xs = x_ref[...]
        for h in range(3):
            yh = mm(xs, w[h]).astype(BF)
            KV[blk, h] = yh[:, :128]
            QQ[blk, h] = yh[:, 128:]

        @pl.when(blk // 2 == p)
        def _():
            for h in range(3):
                send(*l0_kv(blk, h))

        for j in range(2):
            h = fi if j == 0 else 1
            z = mm(sel(h), jnp.concatenate([KV[blk, h], QQ[blk, h]], axis=1)).astype(BF)
            ZKV1[j, blk] = z[0:128, :128]
            ZKV2[j, pl.ds(pl.multiple_of(blk * 64, 64), 64)] = z[128:192, :128]
            ZKV3[j, pl.ds(pl.multiple_of(blk * 32, 32), 32)] = z[192:224, :128]
            ZQ[j, blk] = z[:, 128:]
            send(*l1_kv(blk, j))

    project(tok, zh)

    def fwd(slot_src, slot_dst, sub, n, dev):
        c = rcopy(T.at[slot_src, rows_of(sub)], T.at[slot_dst, rows_of(sub)], ts.at[n], tr.at[n], dev)
        c.start()
        return c

    def share(slot, sub, n):
        c = rcopy(T.at[slot, rows_of(sub)], T.at[slot, rows_of(sub)], cs.at[n], cr.at[n], n_core)
        c.start()
        return c

    def landed(slot, sub, sem):
        arrived(T.at[slot, rows_of(sub)], sem)

    def olo(sub):
        return pl.ds(pl.multiple_of((HALF - lo) + sub * CH, CH), CH)

    def landed_core(slot, sub, sem):
        arrived(T.at[slot, olo(sub)], sem)

    sends = list(own_sends)
    landed(0, zl, tr.at[0])
    sends.append(fwd(0, 1, zl, 2, n_in))
    sends.append(share(0, zl, 0))
    landed(1, 1 - zl, tr.at[2])
    sends.append(fwd(1, 2, 1 - zl, 4, n_out))
    sends.append(share(1, 1 - zl, 2))
    landed(0, 1 - zl, tr.at[1])
    sends.append(fwd(0, 1, 1 - zl, 3, n_in))
    sends.append(share(0, 1 - zl, 1))
    landed_core(0, zl, cr.at[0])
    landed_core(0, 1 - zl, cr.at[1])
    project(T.at[0], g_out)
    landed(2, zl, tr.at[4])
    sends.append(fwd(2, 2, zl, 5, n_in))
    sends.append(share(2, zl, 4))
    landed(1, zl, tr.at[3])
    sends.append(share(1, zl, 3))
    landed_core(1, 1 - zl, cr.at[2])
    landed_core(1, zl, cr.at[3])
    project(T.at[1], (zh - dz + 4) % 4)

    for h in range(3):
        PQ0[h] = jnp.where(low, QQ[2 * p, h], QQ[2 * p + 1, h])
        send(*l0_q(h))

    landed(2, 1 - zl, tr.at[5])
    sends.append(share(2, 1 - zl, 5))
    landed_core(2, zl, cr.at[4])
    landed_core(2, 1 - zl, cr.at[5])
    project(T.at[2], (zh + 2) % 4)

    for t in range(2):
        q = jnp.where(low, ZQ[0, 2 * t], ZQ[0, 2 * t + 1])
        PQ1F[t * 128:(t + 1) * 128] = q[:128]
        PQ2[t] = q[128:192]
        PQ3[t] = q[192:224]
    q = jnp.where(low, ZQ[1, 2 * p], ZQ[1, 2 * p + 1])
    PQ1H[...] = q[:128]
    PQ2[2] = q[128:192]
    PQ3[2] = q[192:224]
    late = [l1_q(0), l1_q(1)]
    for j in range(3):
        late += [l2_kv(j), l2_q(j), l3_kv(j), l3_q(j)]
    for a in late:
        send(*a)

    def attend(Q, K, R, tiles):
        VX[...] = jnp.where(low, jnp.ones((), BF), K[...])

        @pl.loop(0, tiles)
        def _(i):
            r = pl.ds(pl.multiple_of(i * 256, 256), 256)
            q = Q[r]
            qa = jnp.where(low, q, jnp.zeros((), BF))
            qb = jnp.where(low, pltpu.roll(q.astype(F32), 64, 1).astype(BF), jnp.zeros((), BF))
            k = K[...]
            v = VX[...]

            def one(qz):
                s = nt(qz, k)
                m = jnp.max(s, axis=1, keepdims=True)
                e = jnp.exp2((s - m) * (SCALE * LOG2E)).astype(BF)
                return mm(e, v), m

            ua, ma = one(qa)
            ub, mb = one(qb)
            ra = pltpu.roll(ua, 64, 1)
            rb = pltpu.roll(ub, 64, 1)
            tot = jnp.where(low, ua, rb)
            o = jnp.where(low, ra, ub) / tot
            ll = SCALE * jnp.where(low, ma, mb) + jnp.log(tot)
            hi = ll.astype(BF)
            left = ll - hi.astype(F32)
            mid = left.astype(BF)
            tail = (left - mid.astype(F32)).astype(BF)
            l64 = lane & 63
            piece = jnp.where(l64 == 0, hi, jnp.where(l64 == 1, mid, jnp.where(l64 == 2, tail, jnp.zeros((), BF))))
            R[r, 0:128] = o.astype(BF)
            R[r, 128:256] = piece

    arrived(KA, lr.at[0])
    arrived(QA, lr.at[1])
    attend(QA, KA, RA, 4)

    def ret0(xs):
        return (RA.at[pl.ds(pl.multiple_of(xs * 256, 256), 256)], R0.at[x_of], rs.at[xs], rr0.at[x_of], seq_at(y, zh, xs))

    def ret1f(k):
        xs, t = k // 2, k % 2
        return (
            RA.at[pl.ds(pl.multiple_of(xs * 256 + t * 128, 128), 128)],
            R123.at[fi, 0:128],
            rs.at[k],
            rr.at[fi, 0],
            seq_at(y, 2 * t + par, xs),
        )

    def ret1h(xs):
        return (
            RB.at[pl.ds(pl.multiple_of(xs * 128, 128), 128)],
            R123.at[1, 0:128],
            rs.at[8 + xs],
            rr.at[1, 0],
            seq_at(y, zh, xs),
        )

    head_b = jnp.where(x_of == 2, 1, fi)
    zh_b = jnp.where(x_of == 2, zh, 2 * x_of + par)

    def ret2(si):
        return (
            RB.at[pl.ds(pl.multiple_of(si * 64, 64), 64)],
            R123.at[head_b, 128:192],
            rs.at[8 + si],
            rr.at[head_b, 1],
            seq_at(y - y % 2 + si // 4, zh_b, si % 4),
        )

    def ret3(si):
        return (
            RB.at[pl.ds(pl.multiple_of(si * 32, 32), 32)],
            R123.at[head_b, 192:224],
            rs.at[8 + si],
            rr.at[head_b, 2],
            seq_at(si // 4, zh_b, si % 4),
        )

    is_l1 = x_of == 3
    is_l2 = (x_of != 3) & (y % 2 == 0)
    is_l3 = (x_of != 3) & (y == 1)

    def do_all(n, f, act):
        @pl.loop(0, n)
        def _(k):
            act(*f(k))

    @pl.when(x_of != 3)
    def _():
        do_all(4, ret0, send)

    @pl.when(is_l1)
    def _():
        do_all(8, ret1f, send)

    @pl.when(is_l1 | is_l2 | is_l3)
    def _():
        arrived(KB, lr.at[2])
        arrived(QB, lr.at[3])
        attend(QB, KB, RB, 2)

    @pl.when(is_l1)
    def _():
        do_all(4, ret1h, send)

    @pl.when(is_l2)
    def _():
        do_all(8, ret2, send)

    @pl.when(is_l3)
    def _():
        do_all(16, ret3, send)

    R123[:, 224:256] = jnp.zeros((3, 32, 256), BF)
    ji = lax.broadcasted_iota(jnp.int32, (128, 128), 0)
    jo = lax.broadcasted_iota(jnp.int32, (128, 128), 1)
    spread = jnp.where((ji // 64 == jo // 64) & (ji % 64 < 3), 1.0, 0.0).astype(BF)
    row = lax.broadcasted_iota(jnp.int32, (ROWS, 128), 0)
    is_a = par == 0
    lows, highs = [], []
    for h in range(3):
        arrived(R0.at[h], rr0.at[h])
        arrived(R123.at[h, 0:128], rr.at[h, 0])
        arrived(R123.at[h, 128:192], rr.at[h, 1])
        arrived(R123.at[h, 192:224], rr.at[h, 2])
        r0 = R0[h]
        os = [r0[:, :128].astype(F32)]
        logs = [mm(r0[:, 128:], spread)]
        r = R123[h]
        for l, (lo_row, hi_row) in ((1, (0, 128)), (2, (128, 192)), (3, (192, 224))):
            sc = mm(sel_t(h, lo_row, hi_row), r)
            os.append(sc[:, :128])
            lg = mm(sc[:, 128:].astype(BF), spread)
            o_l = offs[l, 3 * par + h] & (2**l - 1)
            logs.append(jnp.where((row & (2**l - 1)) == o_l, lg, ABSENT))
        best = jnp.maximum(jnp.maximum(logs[0], logs[1]), jnp.maximum(logs[2], logs[3]))
        ws = [jnp.exp(v - best) for v in logs]
        den = ws[0] + ws[1] + ws[2] + ws[3]
        num = ws[0] * os[0] + ws[1] * os[1] + ws[2] * os[2] + ws[3] * os[3]
        a = num / den
        ra = pltpu.roll(a, 64, 1)
        lows.append((jnp.where(is_a, a, ra), jnp.where(is_a, ra, a)))
        highs.append((jnp.where(is_a, ra, a), jnp.where(is_a, a, ra)))
    ATT[1, :, 0:128] = jnp.where(low, lows[0][1], highs[1][1]).astype(BF)
    ATT[1, :, 128:256] = lows[2][1].astype(BF)
    partner = (seq_at(y, zh + 1 - 2 * par, x), hd)
    swap = rcopy(ATT.at[1], ATTP, ps, pr, partner)
    swap.start()
    ATT[0, :, 0:128] = jnp.where(low, lows[0][0], highs[1][0]).astype(BF)
    ATT[0, :, 128:256] = lows[2][0].astype(BF)

    mine0 = pl.multiple_of(192 * par, 64)
    other0 = pl.multiple_of(192 * (1 - par), 64)

    def proj(a_ref, start, c):
        cols = slice(c * 512, (c + 1) * 512)
        w01 = wout[pl.ds(start, 128), cols]
        w2 = wout[pl.ds(start + 128, 64), cols]
        return mm(a_ref[:, 0:128], w01) + mm(a_ref[:, 128:192], w2)

    for c in range(3):
        ACC[c] = proj(ATT.at[0], mine0, c)
    swap.wait_recv()
    core_sends = []
    for c in range(3):
        ACC[c] += proj(ATTP, other0, c)
        for zz in range(2):
            SB1[c, zz] = ACC[c, pl.ds(pl.multiple_of(zz * 128 + (1 - core) * 64, 64), 64)].astype(BF)
        cp = rcopy(SB1.at[c], RB1.at[c], s1.at[c], r1.at[c], n_core)
        cp.start()
        core_sends.append(cp)
    in_sends = []
    for c in range(3):
        core_sends[c].wait_recv()
        src = pl.multiple_of((1 - zl) * 128 + core * 64, 64)
        SB2[c] = (ACC[c, pl.ds(src, 64)] + RB1[c, 1 - zl].astype(F32)).astype(BF)
        cp = rcopy(SB2.at[c], RB2.at[c], s2.at[c], r2.at[c], n_in)
        cp.start()
        in_sends.append(cp)
    for c in range(3):
        in_sends[c].wait_recv()
        src = pl.multiple_of(zl * 128 + core * 64, 64)
        tot = ACC[c, pl.ds(src, 64)] + RB1[c, zl].astype(F32) + RB2[c].astype(F32)
        out[:, c * 512:(c + 1) * 512] = tot.astype(BF)

    for c in sends + core_sends + in_sends + [swap]:
        c.wait_send()
    for h in range(3):
        for b in range(2):
            sent(*l0_kv(2 * p + b, h))
        sent(*l0_q(h))
    for j in range(2):
        for blk in range(4):
            sent(*l1_kv(blk, j))
    for a in late:
        sent(*a)

    @pl.when(x_of != 3)
    def _():
        do_all(4, ret0, sent)

    @pl.when(is_l1)
    def _():
        do_all(8, ret1f, sent)
        do_all(4, ret1h, sent)

    @pl.when(is_l2)
    def _():
        do_all(8, ret2, sent)

    @pl.when(is_l3)
    def _():
        do_all(16, ret3, sent)


def local(tokens, query_weight, key_weight, value_weight, offsets, out_weight):
    par = (lax.axis_index("seq") // 4) % 2

    def part(weight):
        return lax.dynamic_slice(weight, (0, 192 * par), (D, 192)).reshape(D, 3, 64)

    q, k, v = part(query_weight), part(key_weight), part(value_weight)
    w = jnp.concatenate([k, v, q, q], axis=2).transpose(1, 0, 2)
    vm = lambda *s: pltpu.VMEM(s, BF)
    dma = lambda *s: pltpu.SemaphoreType.DMA(s)
    return pl.pallas_call(
        body,
        out_shape=jax.ShapeDtypeStruct((64, D), BF),
        in_specs=[pl.BlockSpec(memory_space=pltpu.VMEM)] * 3 + [pl.BlockSpec(memory_space=pltpu.SMEM)],
        out_specs=pl.BlockSpec(memory_space=pltpu.VMEM),
        scratch_shapes=[
            vm(3, 256, D), vm(4, 3, 256, 128), vm(4, 3, 256, 128),
            vm(2, 4, 128, 128), vm(2, 256, 128), vm(2, 128, 128), vm(2, 4, 256, 128),
            vm(3, 256, 128), vm(256, 128), vm(128, 128), vm(3, 64, 128), vm(3, 32, 128),
            vm(2048, 128), vm(1024, 128), vm(2048, 128), vm(512, 128), vm(2048, 128),
            vm(1024, 256), vm(512, 256), vm(3, 256, 256), vm(3, 256, 256),
            vm(2, 256, 256), vm(256, 256), vm(3, 2, 64, 512), vm(3, 2, 64, 512), vm(3, 64, 512), vm(3, 64, 512),
            pltpu.VMEM((3, 256, 512), F32),
            dma(6), dma(6), dma(6), dma(6), dma(10, 4), dma(4), dma(24), dma(3), dma(3, 3), dma(), dma(),
            dma(3), dma(3), dma(3), dma(3), dma(1),
        ],
        compiler_params=pltpu.CompilerParams(has_side_effects=True, vmem_limit_bytes=48 * 1024 * 1024),
    )(tokens, w, out_weight, offsets)


def solution(mesh):
    return jax.shard_map(
        local,
        mesh=mesh,
        in_specs=(
            P("seq", None),
            P(None, "head"),
            P(None, "head"),
            P(None, "head"),
            P(None, "head"),
            P("head", None),
        ),
        out_specs=P(("seq", "head"), None),
        check_vma=False,
    )
```

```python
import jax
import jax.numpy as jnp
from jax import lax
from jax.experimental import pallas as pl
from jax.experimental.pallas import tpu as pltpu
from jax.sharding import PartitionSpec as P

MESH = pl.DeviceIdType.MESH
BF = jnp.bfloat16
F32 = jnp.float32
ROWS = 256
D = 1536
HALF = 128
CH = 32
SCALE = 0.125
LOG2E = 1.4426950408889634
ABSENT = -1e30


def nt(a, b):
    return lax.dot_general(a, b, (((1,), (1,)), ((), ())), preferred_element_type=F32)


def mm(a, b):
    return jnp.dot(a, b, preferred_element_type=F32)


def body(
    tok, wq, wk, wv, wout, offs, out,
    TOK, WIN, W3, WF, T, KV, QQ, ZKV1, ZKV2, ZKV3, ZQ, PQ0, PQ1F, PQ1H, PQ2, PQ3,
    KA, QA, KB, QB, VX, RA, RB, R0, R123, CA, CR, MS, AT, AF,
    win, ts, tr, cs, cr, ls, lr, rs, rr0, rr, ws, wr, fs, fr,
):
    sq = lax.axis_index("seq")
    hd = lax.axis_index("head")
    y = sq // 16
    zh = (sq // 4) % 4
    x = sq % 4
    zl = hd // 2
    core = hd % 2
    par = zh % 2
    p = zh // 2
    fi = 2 * p

    def seq_at(yy, zz, xx):
        return yy * 16 + zz * 4 + xx

    dz = 2 * zl - 1
    g_out = (zh + dz + 4) % 4
    n_out = (seq_at(y, g_out, x), (1 - zl) * 2 + core)
    n_in = (sq, (1 - zl) * 2 + core)
    n_core = (sq, zl * 2 + (1 - core))

    barrier = pltpu.get_barrier_semaphore()

    def hello(dev):
        pl.semaphore_signal(barrier, inc=1, device_id=dev, device_id_type=MESH)

    hello(n_out)
    hello(n_in)
    hello(n_core)
    hello((sq, (1 - zl) * 2 + (1 - core)))

    @pl.loop(1, 16)
    def _(i):
        j = (y * 4 + x + i) % 16
        hello((seq_at(j // 4, zh, j % 4), hd))

    @pl.loop(0, 4)
    def _(i):
        hello((seq_at(y, zh + 1 - 2 * par, x), i))

    start = pl.multiple_of(128 * par, 128)
    loads = [pltpu.make_async_copy(wsrc.at[:, pl.ds(start, 256)], WIN.at[n], win.at[n]) for n, wsrc in enumerate((wk, wv, wq))]
    own_w = pl.ds(pl.multiple_of(384 * hd, 128), 384)
    load_tok = pltpu.make_async_copy(tok, TOK, win.at[3])
    load_wout = pltpu.make_async_copy(wout, WF.at[own_w], win.at[4])
    load_tok.start()
    for c in loads:
        c.start()
    load_wout.start()

    def rcopy(src, dst, ssem, rsem, dev):
        return pltpu.make_async_remote_copy(
            src_ref=src, dst_ref=dst, send_sem=ssem, recv_sem=rsem, device_id=dev, device_id_type=MESH
        )

    def send(src, dst, ssem, rsem, dst_seq):
        @pl.when(dst_seq != sq)
        def _():
            rcopy(src, dst, ssem, rsem, (dst_seq, hd)).start()

        @pl.when(dst_seq == sq)
        def _():
            pltpu.make_async_copy(src, dst, rsem).start()

    def sent(src, dst, ssem, rsem, dst_seq):
        @pl.when(dst_seq != sq)
        def _():
            rcopy(src, dst, ssem, rsem, (dst_seq, hd)).wait_send()

    def arrived(ref, sem):
        pltpu.make_async_copy(ref, ref, sem).wait()

    lane = lax.broadcasted_iota(jnp.int32, (1, 128), 1)
    low = lane < 64

    lo = core * HALF

    def rows_of(sub, k):
        return pl.ds(pl.multiple_of(lo + sub * 64 + k * CH, CH), CH)

    def olo(sub, k):
        return pl.ds(pl.multiple_of((HALF - lo) + sub * 64 + k * CH, CH), CH)

    load_tok.wait()
    pl.semaphore_wait(barrier, 23)
    sends = []
    for n, (sub, k) in enumerate(((1 - zl, 0), (1 - zl, 1), (zl, 0), (zl, 1))):
        c = rcopy(TOK.at[rows_of(sub, k)], T.at[0, rows_of(sub, k)], ts.at[n], tr.at[n], n_out)
        c.start()
        sends.append(c)

    for c in loads:
        c.wait()

    def mover(rows, with_part):
        r = lax.broadcasted_iota(jnp.int32, (rows, 384), 0)
        c = lax.broadcasted_iota(jnp.int32, (rows, 384), 1)
        src = 64 * par + (c // 128) * 64 + c % 64
        if with_part:
            src = src + ((c // 64) % 2) * 256
        return jnp.where(r == src, 1.0, 0.0).astype(BF)

    pkv = mover(512, True)
    pq = mover(256, False)

    @pl.loop(0, 6)
    def _(i):
        r = pl.ds(pl.multiple_of(i * 256, 256), 256)
        wkv = mm(WIN[0, r], pkv[:256]) + mm(WIN[1, r], pkv[256:])
        wqq = mm(WIN[2, r], pq)
        for h in range(3):
            W3[h, r, 0:128] = wkv[:, h * 128:(h + 1) * 128].astype(BF)
            W3[h, r, 128:256] = wqq[:, h * 128:(h + 1) * 128].astype(BF)

    def targets(h, i):
        o1 = offs[1, 3 * par + h] & 1
        o2 = offs[2, 3 * par + h] & 3
        o3 = offs[3, 3 * par + h] & 7
        t1 = i * 2 + o1
        t2 = (i - 128) * 4 + o2
        t3 = (i - 192) * 8 + o3
        return jnp.where(i < 128, t1, jnp.where(i < 192, t2, jnp.where(i < 224, t3, -1)))

    def sel(h):
        i = lax.broadcasted_iota(jnp.int32, (ROWS, ROWS), 0)
        c = lax.broadcasted_iota(jnp.int32, (ROWS, ROWS), 1)
        return jnp.where(targets(h, i) == c, 1.0, 0.0).astype(BF)

    def sel_t(h, first_row, last_row):
        i = lax.broadcasted_iota(jnp.int32, (ROWS, ROWS), 1)
        c = lax.broadcasted_iota(jnp.int32, (ROWS, ROWS), 0)
        hit = (targets(h, i) == c) & (i >= first_row) & (i < last_row)
        return jnp.where(hit, 1.0, 0.0).astype(BF)

    def role_seq(role, yy):
        return seq_at(yy, zh, (role + 2 * core) % 4)

    x_of = (x + 2 * core) % 4

    def at(ref, first_row, n):
        return ref.at[pl.ds(pl.multiple_of(first_row, n), n)]

    s2 = (y % 2) * 4 + x
    s3 = y * 4 + x
    y2 = y - y % 2

    def l0_kv(blk, h):
        b = blk % 2
        return KV.at[blk, h], at(KA, x * 512 + b * 256, 256), ls.at[h, b], lr.at[0], role_seq(h, y)

    def l0_q(h):
        return PQ0.at[h], at(QA, x * 256, 256), ls.at[h, 2], lr.at[1], role_seq(h, y)

    def l1_kv(blk, j):
        dst = at((KA, KB)[j], x * 512 + blk * 128, 128)
        return ZKV1.at[j, blk], dst, ls.at[3 + j, blk], lr.at[2 * j], role_seq(3, y)

    def l2_kv(blk, j):
        return ZKV2.at[j // 2, blk], at(KB, s2 * 256 + blk * 64, 64), ls.at[5 + j, blk], lr.at[2], role_seq(j, y2)

    def l3_kv(blk, j):
        return ZKV3.at[j // 2, blk], at(KB, s3 * 128 + blk * 32, 32), ls.at[8 + j, blk], lr.at[2], role_seq(j, 1)

    def q_f(t):
        return [
            (PQ1F.at[t], at(QA, x * 256 + t * 128, 128), ls.at[11, t], lr.at[1], role_seq(3, y)),
            (PQ2.at[t], at(QB, s2 * 64, 64), ls.at[12, t], lr.at[3], role_seq(t, y2)),
            (PQ3.at[t], at(QB, s3 * 32, 32), ls.at[13, t], lr.at[3], role_seq(t, 1)),
        ]

    def q_h():
        return [
            (PQ1H, at(QB, x * 128, 128), ls.at[11, 2], lr.at[3], role_seq(3, y)),
            (PQ2.at[2], at(QB, s2 * 64, 64), ls.at[12, 2], lr.at[3], role_seq(2, y2)),
            (PQ3.at[2], at(QB, s3 * 32, 32), ls.at[13, 2], lr.at[3], role_seq(2, 1)),
        ]

    def project(x_ref, blk):
        xs = x_ref[...]
        for h in range(3):
            yh = mm(xs, W3[h]).astype(BF)
            KV[blk, h] = yh[:, :128]
            QQ[blk, h] = yh[:, 128:]

        @pl.when(blk // 2 == p)
        def _():
            for h in range(3):
                send(*l0_kv(blk, h))

        for j in range(2):
            h = fi if j == 0 else 1
            z = mm(sel(h), jnp.concatenate([KV[blk, h], QQ[blk, h]], axis=1)).astype(BF)
            ZKV1[j, blk] = z[0:128, :128]
            ZKV2[j, blk] = z[128:192, :128]
            ZKV3[j, blk] = z[192:224, :128]
            ZQ[j, blk] = z[:, 128:]
            send(*l1_kv(blk, j))
        for j in range(3):
            send(*l2_kv(blk, j))
            send(*l3_kv(blk, j))

    def pack_f(t):
        q = jnp.where(low, ZQ[0, 2 * t], ZQ[0, 2 * t + 1])
        PQ1F[t] = q[:128]
        PQ2[t] = q[128:192]
        PQ3[t] = q[192:224]
        for a in q_f(t):
            send(*a)

    def fwd(src_slot, dst_slot, sub, k, n, dev):
        c = rcopy(T.at[src_slot, rows_of(sub, k)], T.at[dst_slot, rows_of(sub, k)], ts.at[n], tr.at[n], dev)
        c.start()
        sends.append(c)

    def share(slot, sub, k, n):
        c = rcopy(T.at[slot, rows_of(sub, k)], T.at[slot, rows_of(sub, k)], cs.at[n], cr.at[n], n_core)
        c.start()
        sends.append(c)

    def landed(slot, sub, k, sem):
        arrived(T.at[slot, rows_of(sub, k)], sem)

    def shared(slot, sub, k, n):
        arrived(T.at[slot, olo(sub, k)], cr.at[n])

    project(TOK, zh)

    for k in range(2):
        landed(0, zl, k, tr.at[k])
        fwd(0, 1, zl, k, 4 + k, n_in)
        share(0, zl, k, k)
    for k in range(2):
        landed(1, 1 - zl, k, tr.at[4 + k])
        fwd(1, 2, 1 - zl, k, 8 + k, n_out)
        share(1, 1 - zl, k, 4 + k)
    for k in range(2):
        landed(0, 1 - zl, k, tr.at[2 + k])
        fwd(0, 1, 1 - zl, k, 6 + k, n_in)
        share(0, 1 - zl, k, 2 + k)
    for k in range(2):
        shared(0, zl, k, k)
        shared(0, 1 - zl, k, 2 + k)
    project(T.at[0], g_out)
    for k in range(2):
        landed(2, zl, k, tr.at[8 + k])
        fwd(2, 2, zl, k, 10 + k, n_in)
        share(2, zl, k, 8 + k)
    for k in range(2):
        landed(1, zl, k, tr.at[6 + k])
        share(1, zl, k, 6 + k)
    for k in range(2):
        shared(1, 1 - zl, k, 4 + k)
        shared(1, zl, k, 6 + k)
    project(T.at[1], (zh - dz + 4) % 4)

    for h in range(3):
        PQ0[h] = jnp.where(low, QQ[2 * p, h], QQ[2 * p + 1, h])
        send(*l0_q(h))
    q = jnp.where(low, ZQ[1, 2 * p], ZQ[1, 2 * p + 1])
    PQ1H[...] = q[:128]
    PQ2[2] = q[128:192]
    PQ3[2] = q[192:224]
    for a in q_h():
        send(*a)
    pack_f(p)

    def attend(Q, K, R, tiles):
        VX[...] = jnp.where(low, jnp.ones((), BF), K[...])

        @pl.loop(0, tiles)
        def _(i):
            r = pl.ds(pl.multiple_of(i * 256, 256), 256)
            q = Q[r]
            qa = jnp.where(low, q, jnp.zeros((), BF))
            qb = jnp.where(low, pltpu.roll(q.astype(F32), 64, 1).astype(BF), jnp.zeros((), BF))
            k = K[...]
            v = VX[...]

            def one(qz):
                s = nt(qz, k)
                m = jnp.max(s, axis=1, keepdims=True)
                e = jnp.exp2((s - m) * (SCALE * LOG2E)).astype(BF)
                return mm(e, v), m

            ua, ma = one(qa)
            ub, mb = one(qb)
            ra = pltpu.roll(ua, 64, 1)
            rb = pltpu.roll(ub, 64, 1)
            tot = jnp.where(low, ua, rb)
            o = jnp.where(low, ra, ub) / tot
            ll = SCALE * jnp.where(low, ma, mb) + jnp.log(tot)
            hi = ll.astype(BF)
            left = ll - hi.astype(F32)
            mid = left.astype(BF)
            tail = (left - mid.astype(F32)).astype(BF)
            l64 = lane & 63
            piece = jnp.where(l64 == 0, hi, jnp.where(l64 == 1, mid, jnp.where(l64 == 2, tail, jnp.zeros((), BF))))
            R[r, 0:128] = o.astype(BF)
            R[r, 128:256] = piece

    def ret0(xs):
        return at(RA, xs * 256, 256), R0.at[x_of], rs.at[xs], rr0.at[x_of], seq_at(y, zh, xs)

    def ret1f(k):
        xs, t = k // 2, k % 2
        dst = seq_at(y, 2 * t + par, xs)
        return at(RA, xs * 256 + t * 128, 128), R123.at[fi, 0:128], rs.at[k], rr.at[fi, 0], dst

    def ret1h(xs):
        return at(RB, xs * 128, 128), R123.at[1, 0:128], rs.at[8 + xs], rr.at[1, 0], seq_at(y, zh, xs)

    head_b = jnp.where(x_of == 2, 1, fi)
    zh_b = jnp.where(x_of == 2, zh, 2 * x_of + par)

    def ret2(si):
        dst = seq_at(y2 + si // 4, zh_b, si % 4)
        return at(RB, si * 64, 64), R123.at[head_b, 128:192], rs.at[8 + si], rr.at[head_b, 1], dst

    def ret3(si):
        dst = seq_at(si // 4, zh_b, si % 4)
        return at(RB, si * 32, 32), R123.at[head_b, 192:224], rs.at[8 + si], rr.at[head_b, 2], dst

    is_l1 = x_of == 3
    is_l2 = (x_of != 3) & (y % 2 == 0)
    is_l3 = (x_of != 3) & (y == 1)

    def do_all(n, f, act):
        @pl.loop(0, n)
        def _(k):
            act(*f(k))

    @pl.when(x_of != 3)
    def _():
        arrived(KA, lr.at[0])
        arrived(QA, lr.at[1])
        attend(QA, KA, RA, 4)
        do_all(4, ret0, send)

    for k in range(2):
        landed(2, 1 - zl, k, tr.at[10 + k])
        share(2, 1 - zl, k, 10 + k)
    for k in range(2):
        shared(2, zl, k, 8 + k)
        shared(2, 1 - zl, k, 10 + k)
    project(T.at[2], (zh + 2) % 4)
    pack_f(1 - p)

    load_wout.wait()

    def w_rows(first_row, n):
        return WF.at[pl.ds(pl.multiple_of(first_row, 64), n)]

    w_core = rcopy(WF.at[own_w], WF.at[own_w], ws.at[0], wr.at[0], n_core)
    w_in = rcopy(w_rows(384 * hd, 192), w_rows(384 * hd, 192), ws.at[1], wr.at[1], n_in)
    w_out = rcopy(w_rows(384 * hd + 192, 192), w_rows(384 * hd + 192, 192), ws.at[2], wr.at[2], n_out)
    for c in (w_core, w_in, w_out):
        c.start()
        sends.append(c)

    @pl.when(is_l1)
    def _():
        arrived(KA, lr.at[0])
        arrived(QA, lr.at[1])
        attend(QA, KA, RA, 4)
        do_all(8, ret1f, send)

    @pl.when(is_l1 | is_l2 | is_l3)
    def _():
        arrived(KB, lr.at[2])
        arrived(QB, lr.at[3])
        attend(QB, KB, RB, 2)

    @pl.when(is_l1)
    def _():
        do_all(4, ret1h, send)

    @pl.when(is_l2)
    def _():
        do_all(8, ret2, send)

    @pl.when(is_l3)
    def _():
        do_all(16, ret3, send)

    hd_in = (1 - zl) * 2 + core
    arrived(w_rows(384 * hd_in, 192), wr.at[1])
    arrived(w_rows(384 * hd_in + 192, 192), wr.at[2])
    w_pass = rcopy(w_rows(384 * hd_in, 384), w_rows(384 * hd_in, 384), ws.at[3], wr.at[3], n_core)
    w_pass.start()
    sends.append(w_pass)

    R123[:, 224:256] = jnp.zeros((3, 32, 256), BF)
    ji = lax.broadcasted_iota(jnp.int32, (128, 128), 0)
    jo = lax.broadcasted_iota(jnp.int32, (128, 128), 1)
    spread = jnp.where((ji // 64 == jo // 64) & (ji % 64 < 3), 1.0, 0.0).astype(BF)
    row = lax.broadcasted_iota(jnp.int32, (ROWS, 128), 0)
    for h in (1, 0, 2):
        arrived(R0.at[h], rr0.at[h])
        arrived(R123.at[h, 0:128], rr.at[h, 0])
        arrived(R123.at[h, 128:192], rr.at[h, 1])
        arrived(R123.at[h, 192:224], rr.at[h, 2])
        r0 = R0[h]
        os = [r0[:, :128].astype(F32)]
        logs = [mm(r0[:, 128:], spread)]
        r = R123[h]
        for l, (lo_row, hi_row) in ((1, (0, 128)), (2, (128, 192)), (3, (192, 224))):
            sc = mm(sel_t(h, lo_row, hi_row), r)
            os.append(sc[:, :128])
            lg = mm(sc[:, 128:].astype(BF), spread)
            o_l = offs[l, 3 * par + h] & (2**l - 1)
            logs.append(jnp.where((row & (2**l - 1)) == o_l, lg, ABSENT))
        best = jnp.maximum(jnp.maximum(logs[0], logs[1]), jnp.maximum(logs[2], logs[3]))
        wts = [jnp.exp(v - best) for v in logs]
        den = wts[0] + wts[1] + wts[2] + wts[3]
        num = wts[0] * os[0] + wts[1] * os[1] + wts[2] * os[2] + wts[3] * os[3]
        a = num / den
        CA[h] = a
        CR[h] = pltpu.roll(a, 64, 1)

    slot = par * 4 + hd
    for b in range(2):
        LO, HI = (CA, CR) if b == 0 else (CR, CA)
        two = jnp.where(low, LO[par], HI[par + 1])
        lo1, hi1 = LO[2 - 2 * par], HI[2 - 2 * par]
        for i in range(4):
            r = i * 64
            MS[b, i, 0:64] = two[r:r + 64].astype(BF)
            MS[b, i, 64:96] = jnp.where(low, lo1[r:r + 32], hi1[r + 32:r + 64]).astype(BF)

    def final(b, i):
        return MS.at[b, i], AT.at[slot], fs.at[b * 4 + i], fr.at[slot], seq_at(y, 2 * p + b, x), i

    @pl.loop(0, 8)
    def _(n):
        src, dst, ssem, rsem, dseq, dhd = final(n // 4, n % 4)

        @pl.when((dseq != sq) | (dhd != hd))
        def _():
            rcopy(src, dst, ssem, rsem, (dseq, dhd)).start()

        @pl.when((dseq == sq) & (dhd == hd))
        def _():
            pltpu.make_async_copy(src, dst, rsem).start()

    arrived(WF.at[pl.ds(pl.multiple_of(384 * (hd + 1 - 2 * core), 128), 384)], wr.at[0])
    arrived(WF.at[pl.ds(pl.multiple_of(384 * (hd_in + 1 - 2 * core), 128), 384)], wr.at[3])

    for i in range(4):
        arrived(AT.at[i], fr.at[i])
        arrived(AT.at[4 + i], fr.at[4 + i])
        e, o = AT[i], AT[4 + i]
        x0 = e[64:96].astype(F32)
        x1 = o[64:96].astype(F32)
        AF[:, i * 384:i * 384 + 128] = e[:64]
        AF[0:32, i * 384 + 128:i * 384 + 256] = jnp.where(low, x0, pltpu.roll(x1, 64, 1)).astype(BF)
        AF[32:64, i * 384 + 128:i * 384 + 256] = jnp.where(low, pltpu.roll(x0, 64, 1), x1).astype(BF)
        AF[:, i * 384 + 256:(i + 1) * 384] = o[:64]
    out[...] = mm(AF[...], WF[...]).astype(BF)

    for c in sends:
        c.wait_send()

    @pl.loop(0, 8)
    def _(n):
        src, dst, ssem, rsem, dseq, dhd = final(n // 4, n % 4)

        @pl.when((dseq != sq) | (dhd != hd))
        def _():
            rcopy(src, dst, ssem, rsem, (dseq, dhd)).wait_send()

    for h in range(3):
        for b in range(2):
            sent(*l0_kv(2 * p + b, h))
        sent(*l0_q(h))

    @pl.loop(0, 4)
    def _(blk):
        for j in range(2):
            sent(*l1_kv(blk, j))
        for j in range(3):
            sent(*l2_kv(blk, j))
            sent(*l3_kv(blk, j))

    for a in q_h() + q_f(0) + q_f(1):
        sent(*a)

    @pl.when(x_of != 3)
    def _():
        do_all(4, ret0, sent)

    @pl.when(is_l1)
    def _():
        do_all(8, ret1f, sent)
        do_all(4, ret1h, sent)

    @pl.when(is_l2)
    def _():
        do_all(8, ret2, sent)

    @pl.when(is_l3)
    def _():
        do_all(16, ret3, sent)


def local(tokens, query_weight, key_weight, value_weight, offsets, out_weight):
    vm = lambda *s: pltpu.VMEM(s, BF)
    dma = lambda *s: pltpu.SemaphoreType.DMA(s)
    return pl.pallas_call(
        body,
        out_shape=jax.ShapeDtypeStruct((64, D), BF),
        in_specs=[pl.BlockSpec(memory_space=pl.ANY)] * 5 + [pl.BlockSpec(memory_space=pltpu.SMEM)],
        out_specs=pl.BlockSpec(memory_space=pltpu.VMEM),
        scratch_shapes=[
            vm(256, D), vm(3, D, 256), vm(3, D, 256), vm(D, D),
            vm(3, 256, D), vm(4, 3, 256, 128), vm(4, 3, 256, 128),
            vm(2, 4, 128, 128), vm(2, 4, 64, 128), vm(2, 4, 32, 128), vm(2, 4, 256, 128),
            vm(3, 256, 128), vm(2, 128, 128), vm(128, 128), vm(3, 64, 128), vm(3, 32, 128),
            vm(2048, 128), vm(1024, 128), vm(2048, 128), vm(512, 128), vm(2048, 128),
            vm(1024, 256), vm(512, 256), vm(3, 256, 256), vm(3, 256, 256),
            pltpu.VMEM((3, 256, 128), F32), pltpu.VMEM((3, 256, 128), F32),
            vm(2, 4, 96, 128), vm(8, 96, 128), vm(64, D),
            dma(5), dma(12), dma(12), dma(12), dma(12), dma(14, 4), dma(4), dma(24), dma(3), dma(3, 3),
            dma(4), dma(4), dma(8), dma(8),
        ],
        compiler_params=pltpu.CompilerParams(
            has_side_effects=True, collective_id=1, vmem_limit_bytes=48 * 1024 * 1024
        ),
    )(tokens, query_weight, key_weight, value_weight, out_weight, offsets)


def solution(mesh):
    return jax.shard_map(
        local,
        mesh=mesh,
        in_specs=(
            P("seq", None),
            P(None, "head"),
            P(None, "head"),
            P(None, "head"),
            P(None, "head"),
            P("head", None),
        ),
        out_specs=P(("seq", "head"), None),
        check_vma=False,
    )
```

```python
import jax
import jax.numpy as jnp
from jax import lax
from jax.experimental import pallas as pl
from jax.experimental.pallas import tpu as pltpu
from jax.sharding import PartitionSpec as P

MESH = pl.DeviceIdType.MESH
BF = jnp.bfloat16
F32 = jnp.float32
ROWS = 256
D = 1536
HALF = 128
SCALE = 0.125
LOG2E = 1.4426950408889634
ABSENT = -1e30


def nt(a, b):
    return lax.dot_general(a, b, (((1,), (1,)), ((), ())), preferred_element_type=F32)


def mm(a, b):
    return jnp.dot(a, b, preferred_element_type=F32)


def body(
    tok, wq, wk, wv, wout, offs, out,
    TOK, WIN, W3, WF, T, KV, QQ, ZKV1, ZKV2, ZKV3, ZQ, PQ0, PQ1F, PQ1H, PQ2, PQ3,
    KA, QA, KB, QB, VX, RA, RB, R0, R123, CA, CR, MS, AT, AF,
    win, ts, tr, cs, cr, ls, lr, rs, rr0, rr, ws, wr, fs, fr,
):
    sq = lax.axis_index("seq")
    hd = lax.axis_index("head")
    y = sq // 16
    zh = (sq // 4) % 4
    x = sq % 4
    zl = hd // 2
    core = hd % 2
    par = zh % 2
    p = zh // 2
    fi = 2 * p

    def seq_at(yy, zz, xx):
        return yy * 16 + zz * 4 + xx

    dz = 2 * zl - 1
    g_out = (zh + dz + 4) % 4
    n_out = (seq_at(y, g_out, x), (1 - zl) * 2 + core)
    n_in = (sq, (1 - zl) * 2 + core)
    n_core = (sq, zl * 2 + (1 - core))

    barrier = pltpu.get_barrier_semaphore()

    def hello(dev):
        pl.semaphore_signal(barrier, inc=1, device_id=dev, device_id_type=MESH)

    hello(n_out)
    hello(n_in)
    hello(n_core)
    hello((sq, (1 - zl) * 2 + (1 - core)))

    @pl.loop(1, 16)
    def _(i):
        j = (y * 4 + x + i) % 16
        hello((seq_at(j // 4, zh, j % 4), hd))

    @pl.loop(0, 4)
    def _(i):
        hello((seq_at(y, zh + 1 - 2 * par, x), i))

    start = pl.multiple_of(128 * par, 128)
    loads = [pltpu.make_async_copy(wsrc.at[:, pl.ds(start, 256)], WIN.at[n], win.at[n]) for n, wsrc in enumerate((wk, wv, wq))]
    own_w = pl.ds(pl.multiple_of(384 * hd, 128), 384)
    load_tok = pltpu.make_async_copy(tok, TOK, win.at[3])
    load_wout = pltpu.make_async_copy(wout, WF.at[own_w], win.at[4])
    load_tok.start()
    for c in loads:
        c.start()
    load_wout.start()

    def rcopy(src, dst, ssem, rsem, dev):
        return pltpu.make_async_remote_copy(
            src_ref=src, dst_ref=dst, send_sem=ssem, recv_sem=rsem, device_id=dev, device_id_type=MESH
        )

    def send(src, dst, ssem, rsem, dst_seq):
        @pl.when(dst_seq != sq)
        def _():
            rcopy(src, dst, ssem, rsem, (dst_seq, hd)).start()

        @pl.when(dst_seq == sq)
        def _():
            pltpu.make_async_copy(src, dst, rsem).start()

    def sent(src, dst, ssem, rsem, dst_seq):
        @pl.when(dst_seq != sq)
        def _():
            rcopy(src, dst, ssem, rsem, (dst_seq, hd)).wait_send()

    def arrived(ref, sem):
        pltpu.make_async_copy(ref, ref, sem).wait()

    lane = lax.broadcasted_iota(jnp.int32, (1, 128), 1)
    low = lane < 64

    lo = core * HALF

    FAR = [(i * 16, 16) for i in range(4)]
    NEAR = [(i * 32, 32) for i in range(2)]

    def rows_of(sub, part):
        return pl.ds(pl.multiple_of(lo + sub * 64 + part[0], part[1]), part[1])

    def other_rows(sub):
        return pl.ds(pl.multiple_of(HALF - lo + sub * 64, 64), 64)

    load_tok.wait()
    pl.semaphore_wait(barrier, 23)
    sends = []

    def own(sub, part, n):
        c = rcopy(TOK.at[rows_of(sub, part)], T.at[0, rows_of(sub, part)], ts.at[n], tr.at[n], n_out)
        c.start()
        sends.append(c)

    for k, part in enumerate(FAR):
        own(1 - zl, part, k)

    for c in loads:
        c.wait()

    def mover(rows, with_part):
        r = lax.broadcasted_iota(jnp.int32, (rows, 384), 0)
        c = lax.broadcasted_iota(jnp.int32, (rows, 384), 1)
        src = 64 * par + (c // 128) * 64 + c % 64
        if with_part:
            src = src + ((c // 64) % 2) * 256
        return jnp.where(r == src, 1.0, 0.0).astype(BF)

    pkv = mover(512, True)
    pq = mover(256, False)

    @pl.loop(0, 6)
    def _(i):
        r = pl.ds(pl.multiple_of(i * 256, 256), 256)
        wkv = mm(WIN[0, r], pkv[:256]) + mm(WIN[1, r], pkv[256:])
        wqq = mm(WIN[2, r], pq)
        for h in range(3):
            W3[h, r, 0:128] = wkv[:, h * 128:(h + 1) * 128].astype(BF)
            W3[h, r, 128:256] = wqq[:, h * 128:(h + 1) * 128].astype(BF)

    def targets(h, i):
        o1 = offs[1, 3 * par + h] & 1
        o2 = offs[2, 3 * par + h] & 3
        o3 = offs[3, 3 * par + h] & 7
        t1 = i * 2 + o1
        t2 = (i - 128) * 4 + o2
        t3 = (i - 192) * 8 + o3
        return jnp.where(i < 128, t1, jnp.where(i < 192, t2, jnp.where(i < 224, t3, -1)))

    def sel(h):
        i = lax.broadcasted_iota(jnp.int32, (ROWS, ROWS), 0)
        c = lax.broadcasted_iota(jnp.int32, (ROWS, ROWS), 1)
        return jnp.where(targets(h, i) == c, 1.0, 0.0).astype(BF)

    def sel_t(h, first_row, last_row):
        i = lax.broadcasted_iota(jnp.int32, (ROWS, ROWS), 1)
        c = lax.broadcasted_iota(jnp.int32, (ROWS, ROWS), 0)
        hit = (targets(h, i) == c) & (i >= first_row) & (i < last_row)
        return jnp.where(hit, 1.0, 0.0).astype(BF)

    def role_seq(role, yy):
        return seq_at(yy, zh, (role + 2 * core) % 4)

    x_of = (x + 2 * core) % 4

    def at(ref, first_row, n):
        return ref.at[pl.ds(pl.multiple_of(first_row, n), n)]

    s2 = (y % 2) * 4 + x
    s3 = y * 4 + x
    y2 = y - y % 2

    def l0_kv(blk, h):
        b = blk % 2
        return KV.at[blk, h], at(KA, x * 512 + b * 256, 256), ls.at[h, b], lr.at[0], role_seq(h, y)

    def l0_q(h):
        return PQ0.at[h], at(QA, x * 256, 256), ls.at[h, 2], lr.at[1], role_seq(h, y)

    def l1_kv(blk, j):
        dst = at((KA, KB)[j], x * 512 + blk * 128, 128)
        return ZKV1.at[j, blk], dst, ls.at[3 + j, blk], lr.at[2 * j], role_seq(3, y)

    def l2_kv(blk, j):
        return ZKV2.at[j // 2, blk], at(KB, s2 * 256 + blk * 64, 64), ls.at[5 + j, blk], lr.at[2], role_seq(j, y2)

    def l3_kv(blk, j):
        return ZKV3.at[j // 2, blk], at(KB, s3 * 128 + blk * 32, 32), ls.at[8 + j, blk], lr.at[2], role_seq(j, 1)

    def q_f(t):
        return [
            (PQ1F.at[t], at(QA, x * 256 + t * 128, 128), ls.at[11, t], lr.at[1], role_seq(3, y)),
            (PQ2.at[t], at(QB, s2 * 64, 64), ls.at[12, t], lr.at[3], role_seq(t, y2)),
            (PQ3.at[t], at(QB, s3 * 32, 32), ls.at[13, t], lr.at[3], role_seq(t, 1)),
        ]

    def q_h():
        return [
            (PQ1H, at(QB, x * 128, 128), ls.at[11, 2], lr.at[3], role_seq(3, y)),
            (PQ2.at[2], at(QB, s2 * 64, 64), ls.at[12, 2], lr.at[3], role_seq(2, y2)),
            (PQ3.at[2], at(QB, s3 * 32, 32), ls.at[13, 2], lr.at[3], role_seq(2, 1)),
        ]

    def project(x_ref, blk):
        xs = x_ref[...]
        for h in range(3):
            yh = mm(xs, W3[h]).astype(BF)
            KV[blk, h] = yh[:, :128]
            QQ[blk, h] = yh[:, 128:]

        @pl.when(blk // 2 == p)
        def _():
            for h in range(3):
                send(*l0_kv(blk, h))

        for j in range(2):
            h = fi if j == 0 else 1
            z = mm(sel(h), jnp.concatenate([KV[blk, h], QQ[blk, h]], axis=1)).astype(BF)
            ZKV1[j, blk] = z[0:128, :128]
            ZKV2[j, blk] = z[128:192, :128]
            ZKV3[j, blk] = z[192:224, :128]
            ZQ[j, blk] = z[:, 128:]
            send(*l1_kv(blk, j))
        for j in range(3):
            send(*l2_kv(blk, j))
            send(*l3_kv(blk, j))

    def pack_f(t):
        q = jnp.where(low, ZQ[0, 2 * t], ZQ[0, 2 * t + 1])
        PQ1F[t] = q[:128]
        PQ2[t] = q[128:192]
        PQ3[t] = q[192:224]
        for a in q_f(t):
            send(*a)

    def fwd(src_slot, dst_slot, sub, part, n, dev):
        c = rcopy(T.at[src_slot, rows_of(sub, part)], T.at[dst_slot, rows_of(sub, part)], ts.at[n], tr.at[n], dev)
        c.start()
        sends.append(c)

    def share(slot, sub, n):
        r = rows_of(sub, (0, 64))
        c = rcopy(T.at[slot, r], T.at[slot, r], cs.at[n], cr.at[n], n_core)
        c.start()
        sends.append(c)

    def landed(slot, sub, part, n):
        arrived(T.at[slot, rows_of(sub, part)], tr.at[n])

    def shared(slot, sub, n):
        arrived(T.at[slot, other_rows(sub)], cr.at[n])

    project(TOK, zh)

    for k, part in enumerate(FAR):
        landed(0, zl, part, k)
        fwd(0, 1, zl, part, 6 + k, n_in)
    for k, part in enumerate(NEAR):
        own(zl, part, 4 + k)
    share(0, zl, 0)
    for k, part in enumerate(FAR):
        landed(1, 1 - zl, part, 6 + k)
        fwd(1, 2, 1 - zl, part, 12 + k, n_out)
    share(1, 1 - zl, 2)
    for k, part in enumerate(NEAR):
        landed(0, 1 - zl, part, 4 + k)
        fwd(0, 1, 1 - zl, part, 10 + k, n_in)
    share(0, 1 - zl, 1)
    shared(0, zl, 0)
    shared(0, 1 - zl, 1)
    project(T.at[0], g_out)
    for k, part in enumerate(FAR):
        landed(2, zl, part, 12 + k)
        fwd(2, 2, zl, part, 16 + k, n_in)
    share(2, zl, 4)
    for k, part in enumerate(NEAR):
        landed(1, zl, part, 10 + k)
    share(1, zl, 3)
    shared(1, 1 - zl, 2)
    shared(1, zl, 3)
    project(T.at[1], (zh - dz + 4) % 4)

    for h in range(3):
        PQ0[h] = jnp.where(low, QQ[2 * p, h], QQ[2 * p + 1, h])
        send(*l0_q(h))
    q = jnp.where(low, ZQ[1, 2 * p], ZQ[1, 2 * p + 1])
    PQ1H[...] = q[:128]
    PQ2[2] = q[128:192]
    PQ3[2] = q[192:224]
    for a in q_h():
        send(*a)
    pack_f(p)

    def attend(Q, K, R, tiles):
        VX[...] = jnp.where(low, jnp.ones((), BF), K[...])

        @pl.loop(0, tiles)
        def _(i):
            r = pl.ds(pl.multiple_of(i * 256, 256), 256)
            q = Q[r]
            qa = jnp.where(low, q, jnp.zeros((), BF))
            qb = jnp.where(low, pltpu.roll(q.astype(F32), 64, 1).astype(BF), jnp.zeros((), BF))
            k = K[...]
            v = VX[...]

            sa, sb = nt(qa, k), nt(qb, k)
            ma = jnp.max(sa, axis=1, keepdims=True)
            mb = jnp.max(sb, axis=1, keepdims=True)
            ua = mm(jnp.exp2((sa - ma) * (SCALE * LOG2E)).astype(BF), v)
            ub = mm(jnp.exp2((sb - mb) * (SCALE * LOG2E)).astype(BF), v)
            ra = pltpu.roll(ua, 64, 1)
            rb = pltpu.roll(ub, 64, 1)
            tot = jnp.where(low, ua, rb)
            o = jnp.where(low, ra, ub) / tot
            ll = SCALE * jnp.where(low, ma, mb) + jnp.log(tot)
            hi = ll.astype(BF)
            left = ll - hi.astype(F32)
            mid = left.astype(BF)
            tail = (left - mid.astype(F32)).astype(BF)
            l64 = lane & 63
            piece = jnp.where(l64 == 0, hi, jnp.where(l64 == 1, mid, jnp.where(l64 == 2, tail, jnp.zeros((), BF))))
            R[r, 0:128] = o.astype(BF)
            R[r, 128:256] = piece

    def ret0(xs):
        return at(RA, xs * 256, 256), R0.at[x_of], rs.at[xs], rr0.at[x_of], seq_at(y, zh, xs)

    def ret1f(k):
        xs, t = k // 2, k % 2
        dst = seq_at(y, 2 * t + par, xs)
        return at(RA, xs * 256 + t * 128, 128), R123.at[fi, 0:128], rs.at[k], rr.at[fi, 0], dst

    def ret1h(xs):
        return at(RB, xs * 128, 128), R123.at[1, 0:128], rs.at[8 + xs], rr.at[1, 0], seq_at(y, zh, xs)

    head_b = jnp.where(x_of == 2, 1, fi)
    zh_b = jnp.where(x_of == 2, zh, 2 * x_of + par)

    def ret2(si):
        dst = seq_at(y2 + si // 4, zh_b, si % 4)
        return at(RB, si * 64, 64), R123.at[head_b, 128:192], rs.at[8 + si], rr.at[head_b, 1], dst

    def ret3(si):
        dst = seq_at(si // 4, zh_b, si % 4)
        return at(RB, si * 32, 32), R123.at[head_b, 192:224], rs.at[8 + si], rr.at[head_b, 2], dst

    is_l1 = x_of == 3
    is_l2 = (x_of != 3) & (y % 2 == 0)
    is_l3 = (x_of != 3) & (y == 1)

    def do_all(n, f, act):
        @pl.loop(0, n)
        def _(k):
            act(*f(k))

    for k, part in enumerate(FAR):
        landed(2, 1 - zl, part, 16 + k)
    share(2, 1 - zl, 5)
    shared(2, zl, 4)
    shared(2, 1 - zl, 5)
    project(T.at[2], (zh + 2) % 4)
    pack_f(1 - p)

    load_wout.wait()

    def w_rows(first_row, n):
        return WF.at[pl.ds(pl.multiple_of(first_row, 64), n)]

    w_core = rcopy(WF.at[own_w], WF.at[own_w], ws.at[0], wr.at[0], n_core)
    w_in = rcopy(w_rows(384 * hd, 192), w_rows(384 * hd, 192), ws.at[1], wr.at[1], n_in)
    w_out = rcopy(w_rows(384 * hd + 192, 192), w_rows(384 * hd + 192, 192), ws.at[2], wr.at[2], n_out)
    for c in (w_core, w_in, w_out):
        c.start()
        sends.append(c)

    @pl.when(x_of != 3)
    def _():
        arrived(KA, lr.at[0])
        arrived(QA, lr.at[1])
        attend(QA, KA, RA, 4)
        do_all(4, ret0, send)

    @pl.when(is_l1)
    def _():
        arrived(KA, lr.at[0])
        arrived(QA, lr.at[1])
        attend(QA, KA, RA, 4)
        do_all(8, ret1f, send)

    @pl.when(is_l1 | is_l2 | is_l3)
    def _():
        arrived(KB, lr.at[2])
        arrived(QB, lr.at[3])
        attend(QB, KB, RB, 2)

    @pl.when(is_l1)
    def _():
        do_all(4, ret1h, send)

    @pl.when(is_l2)
    def _():
        do_all(8, ret2, send)

    @pl.when(is_l3)
    def _():
        do_all(16, ret3, send)

    hd_in = (1 - zl) * 2 + core
    arrived(w_rows(384 * hd_in, 192), wr.at[1])
    arrived(w_rows(384 * hd_in + 192, 192), wr.at[2])
    w_pass = rcopy(w_rows(384 * hd_in, 384), w_rows(384 * hd_in, 384), ws.at[3], wr.at[3], n_core)
    w_pass.start()
    sends.append(w_pass)

    R123[:, 224:256] = jnp.zeros((3, 32, 256), BF)
    ji = lax.broadcasted_iota(jnp.int32, (128, 128), 0)
    jo = lax.broadcasted_iota(jnp.int32, (128, 128), 1)
    spread = jnp.where((ji // 64 == jo // 64) & (ji % 64 < 3), 1.0, 0.0).astype(BF)
    row = lax.broadcasted_iota(jnp.int32, (ROWS, 128), 0)
    for h in (1, 0, 2):
        arrived(R0.at[h], rr0.at[h])
        arrived(R123.at[h, 0:128], rr.at[h, 0])
        arrived(R123.at[h, 128:192], rr.at[h, 1])
        arrived(R123.at[h, 192:224], rr.at[h, 2])
        r0 = R0[h]
        os = [r0[:, :128].astype(F32)]
        logs = [mm(r0[:, 128:], spread)]
        r = R123[h]
        for l, (lo_row, hi_row) in ((1, (0, 128)), (2, (128, 192)), (3, (192, 224))):
            sc = mm(sel_t(h, lo_row, hi_row), r)
            os.append(sc[:, :128])
            lg = mm(sc[:, 128:].astype(BF), spread)
            o_l = offs[l, 3 * par + h] & (2**l - 1)
            logs.append(jnp.where((row & (2**l - 1)) == o_l, lg, ABSENT))
        best = jnp.maximum(jnp.maximum(logs[0], logs[1]), jnp.maximum(logs[2], logs[3]))
        wts = [jnp.exp(v - best) for v in logs]
        den = wts[0] + wts[1] + wts[2] + wts[3]
        num = wts[0] * os[0] + wts[1] * os[1] + wts[2] * os[2] + wts[3] * os[3]
        a = num / den
        CA[h] = a
        CR[h] = pltpu.roll(a, 64, 1)

    slot = par * 4 + hd
    for b in range(2):
        LO, HI = (CA, CR) if b == 0 else (CR, CA)
        two = jnp.where(low, LO[par], HI[par + 1])
        lo1, hi1 = LO[2 - 2 * par], HI[2 - 2 * par]
        for i in range(4):
            r = i * 64
            MS[b, i, 0:64] = two[r:r + 64].astype(BF)
            MS[b, i, 64:96] = jnp.where(low, lo1[r:r + 32], hi1[r + 32:r + 64]).astype(BF)

    def final(b, i):
        return MS.at[b, i], AT.at[slot], fs.at[b * 4 + i], fr.at[slot], seq_at(y, 2 * p + b, x), i

    @pl.loop(0, 8)
    def _(n):
        src, dst, ssem, rsem, dseq, dhd = final(n // 4, n % 4)

        @pl.when((dseq != sq) | (dhd != hd))
        def _():
            rcopy(src, dst, ssem, rsem, (dseq, dhd)).start()

        @pl.when((dseq == sq) & (dhd == hd))
        def _():
            pltpu.make_async_copy(src, dst, rsem).start()

    arrived(WF.at[pl.ds(pl.multiple_of(384 * (hd + 1 - 2 * core), 128), 384)], wr.at[0])
    arrived(WF.at[pl.ds(pl.multiple_of(384 * (hd_in + 1 - 2 * core), 128), 384)], wr.at[3])

    for i in range(4):
        arrived(AT.at[i], fr.at[i])
        arrived(AT.at[4 + i], fr.at[4 + i])
        e, o = AT[i], AT[4 + i]
        x0 = e[64:96].astype(F32)
        x1 = o[64:96].astype(F32)
        AF[:, i * 384:i * 384 + 128] = e[:64]
        AF[0:32, i * 384 + 128:i * 384 + 256] = jnp.where(low, x0, pltpu.roll(x1, 64, 1)).astype(BF)
        AF[32:64, i * 384 + 128:i * 384 + 256] = jnp.where(low, pltpu.roll(x0, 64, 1), x1).astype(BF)
        AF[:, i * 384 + 256:(i + 1) * 384] = o[:64]
    out[...] = mm(AF[...], WF[...]).astype(BF)

    for c in sends:
        c.wait_send()

    @pl.loop(0, 8)
    def _(n):
        src, dst, ssem, rsem, dseq, dhd = final(n // 4, n % 4)

        @pl.when((dseq != sq) | (dhd != hd))
        def _():
            rcopy(src, dst, ssem, rsem, (dseq, dhd)).wait_send()

    for h in range(3):
        for b in range(2):
            sent(*l0_kv(2 * p + b, h))
        sent(*l0_q(h))

    @pl.loop(0, 4)
    def _(blk):
        for j in range(2):
            sent(*l1_kv(blk, j))
        for j in range(3):
            sent(*l2_kv(blk, j))
            sent(*l3_kv(blk, j))

    for a in q_h() + q_f(0) + q_f(1):
        sent(*a)

    @pl.when(x_of != 3)
    def _():
        do_all(4, ret0, sent)

    @pl.when(is_l1)
    def _():
        do_all(8, ret1f, sent)
        do_all(4, ret1h, sent)

    @pl.when(is_l2)
    def _():
        do_all(8, ret2, sent)

    @pl.when(is_l3)
    def _():
        do_all(16, ret3, sent)


def local(tokens, query_weight, key_weight, value_weight, offsets, out_weight):
    vm = lambda *s: pltpu.VMEM(s, BF)
    dma = lambda *s: pltpu.SemaphoreType.DMA(s)
    return pl.pallas_call(
        body,
        out_shape=jax.ShapeDtypeStruct((64, D), BF),
        in_specs=[pl.BlockSpec(memory_space=pl.ANY)] * 5 + [pl.BlockSpec(memory_space=pltpu.SMEM)],
        out_specs=pl.BlockSpec(memory_space=pltpu.VMEM),
        scratch_shapes=[
            vm(256, D), vm(3, D, 256), vm(3, D, 256), vm(D, D),
            vm(3, 256, D), vm(4, 3, 256, 128), vm(4, 3, 256, 128),
            vm(2, 4, 128, 128), vm(2, 4, 64, 128), vm(2, 4, 32, 128), vm(2, 4, 256, 128),
            vm(3, 256, 128), vm(2, 128, 128), vm(128, 128), vm(3, 64, 128), vm(3, 32, 128),
            vm(2048, 128), vm(1024, 128), vm(2048, 128), vm(512, 128), vm(2048, 128),
            vm(1024, 256), vm(512, 256), vm(3, 256, 256), vm(3, 256, 256),
            pltpu.VMEM((3, 256, 128), F32), pltpu.VMEM((3, 256, 128), F32),
            vm(2, 4, 96, 128), vm(8, 96, 128), vm(64, D),
            dma(5), dma(20), dma(20), dma(6), dma(6), dma(14, 4), dma(4), dma(24), dma(3), dma(3, 3),
            dma(4), dma(4), dma(8), dma(8),
        ],
        compiler_params=pltpu.CompilerParams(
            has_side_effects=True, collective_id=1, vmem_limit_bytes=62 * 1024 * 1024
        ),
    )(tokens, query_weight, key_weight, value_weight, out_weight, offsets)


def solution(mesh):
    return jax.shard_map(
        local,
        mesh=mesh,
        in_specs=(
            P("seq", None),
            P(None, "head"),
            P(None, "head"),
            P(None, "head"),
            P(None, "head"),
            P("head", None),
        ),
        out_specs=P(("seq", "head"), None),
        check_vma=False,
    )
```

```python
import jax
import jax.numpy as jnp
from jax import lax
from jax.experimental import pallas as pl
from jax.experimental.pallas import tpu as pltpu
from jax.sharding import PartitionSpec as P

MESH = pl.DeviceIdType.MESH
BF = jnp.bfloat16
F32 = jnp.float32
ROWS = 256
D = 1536
HALF = 128
SCALE = 0.125
LOG2E = 1.4426950408889634
ABSENT = -1e30


def nt(a, b):
    return lax.dot_general(a, b, (((1,), (1,)), ((), ())), preferred_element_type=F32)


def mm(a, b):
    return jnp.dot(a, b, preferred_element_type=F32)


def body(
    tok, wq, wk, wv, wout, offs, out,
    TOK, WIN, W3, WF, T, KV, QQ, ZKV1, ZKV2, ZKV3, ZQ, PQ0, PQ1, PQ2, PQ3,
    KA, QA, KB, QB, KC, QC, VX, RA, RB, RC, R0, R123, CA, CR, MS, AT, AF,
    win, ts, tr, cs, cr, ls, lr, rs, rr0, rr, ws, wr, fs, fr,
    sxa, sya, sxb,
):
    sq = lax.axis_index("seq")
    hd = lax.axis_index("head")
    y = sq // 16
    zh = (sq // 4) % 4
    x = sq % 4
    zl = hd // 2
    core = hd % 2
    par = zh % 2
    p = zh // 2

    def seq_at(yy, zz, xx):
        return yy * 16 + zz * 4 + xx

    dz = 2 * zl - 1
    g_out = (zh + dz + 4) % 4
    n_out = (seq_at(y, g_out, x), (1 - zl) * 2 + core)
    n_in = (sq, (1 - zl) * 2 + core)
    n_core = (sq, zl * 2 + (1 - core))

    barrier = pltpu.get_barrier_semaphore()

    def hello(dev):
        pl.semaphore_signal(barrier, inc=1, device_id=dev, device_id_type=MESH)

    hello(n_out)
    hello(n_in)
    hello(n_core)
    x_next = [(seq_at(y, zh, (x + d) % 4), hd) for d in (1, 3)]
    y_next = [(seq_at((y + d) % 4, zh, x), hd) for d in (1, 3)]
    for dev in x_next + y_next:
        hello(dev)

    def tell(sem, devs):
        for dev in devs:
            pl.semaphore_signal(sem, inc=1, device_id=dev, device_id_type=MESH)

    start = pl.multiple_of(128 * par, 128)
    loads = [pltpu.make_async_copy(wsrc.at[:, pl.ds(start, 256)], WIN.at[n], win.at[n]) for n, wsrc in enumerate((wk, wv, wq))]
    own_w = pl.ds(pl.multiple_of(384 * hd, 128), 384)
    load_tok = pltpu.make_async_copy(tok, TOK, win.at[3])
    load_wout = pltpu.make_async_copy(wout, WF.at[own_w], win.at[4])
    load_tok.start()
    for c in loads:
        c.start()
    load_wout.start()

    def rcopy(src, dst, ssem, rsem, dev):
        return pltpu.make_async_remote_copy(
            src_ref=src, dst_ref=dst, send_sem=ssem, recv_sem=rsem, device_id=dev, device_id_type=MESH
        )

    def send(src, dst, ssem, rsem, dst_seq):
        @pl.when(dst_seq != sq)
        def _():
            rcopy(src, dst, ssem, rsem, (dst_seq, hd)).start()

        @pl.when(dst_seq == sq)
        def _():
            pltpu.make_async_copy(src, dst, rsem).start()

    def sent(src, dst, ssem, rsem, dst_seq):
        @pl.when(dst_seq != sq)
        def _():
            rcopy(src, dst, ssem, rsem, (dst_seq, hd)).wait_send()

    def arrived(ref, sem):
        pltpu.make_async_copy(ref, ref, sem).wait()

    lane = lax.broadcasted_iota(jnp.int32, (1, 128), 1)
    low = lane < 64

    lo = core * HALF

    FAR = [(i * 16, 16) for i in range(4)]
    NEAR = [(i * 32, 32) for i in range(2)]

    def rows_of(sub, part):
        return pl.ds(pl.multiple_of(lo + sub * 64 + part[0], part[1]), part[1])

    def other_rows(sub):
        return pl.ds(pl.multiple_of(HALF - lo + sub * 64, 64), 64)

    load_tok.wait()
    pl.semaphore_wait(barrier, 7)
    sends = []

    def own(sub, part, n):
        c = rcopy(TOK.at[rows_of(sub, part)], T.at[0, rows_of(sub, part)], ts.at[n], tr.at[n], n_out)
        c.start()
        sends.append(c)

    for k, part in enumerate(FAR):
        own(1 - zl, part, k)

    tell(sxa, x_next)

    for c in loads:
        c.wait()

    def mover(rows, with_part):
        r = lax.broadcasted_iota(jnp.int32, (rows, 384), 0)
        c = lax.broadcasted_iota(jnp.int32, (rows, 384), 1)
        src = 64 * par + (c // 128) * 64 + c % 64
        if with_part:
            src = src + ((c // 64) % 2) * 256
        return jnp.where(r == src, 1.0, 0.0).astype(BF)

    pkv = mover(512, True)
    pq = mover(256, False)

    @pl.loop(0, 6)
    def _(i):
        r = pl.ds(pl.multiple_of(i * 256, 256), 256)
        wkv = mm(WIN[0, r], pkv[:256]) + mm(WIN[1, r], pkv[256:])
        wqq = mm(WIN[2, r], pq)
        for h in range(3):
            W3[h, r, 0:128] = wkv[:, h * 128:(h + 1) * 128].astype(BF)
            W3[h, r, 128:256] = wqq[:, h * 128:(h + 1) * 128].astype(BF)

    def targets(h, i):
        o1 = offs[1, 3 * par + h] & 1
        o2 = offs[2, 3 * par + h] & 3
        o3 = offs[3, 3 * par + h] & 7
        t1 = i * 2 + o1
        t2 = (i - 128) * 4 + o2
        t3 = (i - 192) * 8 + o3
        return jnp.where(i < 128, t1, jnp.where(i < 192, t2, jnp.where(i < 224, t3, -1)))

    def sel(h):
        i = lax.broadcasted_iota(jnp.int32, (ROWS, ROWS), 0)
        c = lax.broadcasted_iota(jnp.int32, (ROWS, ROWS), 1)
        return jnp.where(targets(h, i) == c, 1.0, 0.0).astype(BF)

    def sel_t(h, first_row, last_row):
        i = lax.broadcasted_iota(jnp.int32, (ROWS, ROWS), 1)
        c = lax.broadcasted_iota(jnp.int32, (ROWS, ROWS), 0)
        hit = (targets(h, i) == c) & (i >= first_row) & (i < last_row)
        return jnp.where(hit, 1.0, 0.0).astype(BF)

    def role_seq(role, yy):
        return seq_at(yy, zh, (role + 2 * core) % 4)

    x_of = (x + 2 * core) % 4

    def at(ref, first_row, n):
        return ref.at[pl.ds(pl.multiple_of(first_row, n), n)]

    s2 = (y % 2) * 4 + x
    s3 = y * 4 + x
    y2 = y - y % 2

    L2_AT = ((0, 0), (0, 1), (1, 0))
    L3_AT = ((3, 1), (3, 3), (2, 0))

    def l0_kv(blk, h):
        b = blk % 2
        return KV.at[blk, h], at(KA, x * 512 + b * 256, 256), ls.at[h, b], lr.at[0], role_seq(h, y)

    def l1_kv(blk, h):
        return ZKV1.at[h, blk], at(KB, x * 512 + blk * 128, 128), ls.at[3 + h, blk], lr.at[2], role_seq(h, y)

    def l2_kv(blk, h):
        dy, c = L2_AT[h]
        dst = at((KB, KC)[c], s2 * 256 + blk * 64, 64)
        return ZKV2.at[h, blk], dst, ls.at[6 + h, blk], lr.at[2 + 2 * c], role_seq(3, y2 + dy)

    def l3_kv(blk, h):
        role, yy = L3_AT[h]
        return ZKV3.at[h, blk], at(KC, s3 * 128 + blk * 32, 32), ls.at[9 + h, blk], lr.at[4], role_seq(role, yy)

    def queries(h):
        dy, c = L2_AT[h]
        role, yy = L3_AT[h]
        return [
            (PQ0.at[h], at(QA, x * 256, 256), ls.at[h, 2], lr.at[1], role_seq(h, y)),
            (PQ1.at[h], at(QB, x * 128, 128), ls.at[12 + h, 0], lr.at[3], role_seq(h, y)),
            (PQ2.at[h], at((QB, QC)[c], s2 * 64, 64), ls.at[12 + h, 1], lr.at[3 + 2 * c], role_seq(3, y2 + dy)),
            (PQ3.at[h], at(QC, s3 * 32, 32), ls.at[12 + h, 2], lr.at[5], role_seq(role, yy)),
        ]

    def project(x_ref, blk):
        xs = x_ref[...]
        for h in range(3):
            yh = mm(xs, W3[h]).astype(BF)
            KV[blk, h] = yh[:, :128]
            QQ[blk, h] = yh[:, 128:]

        @pl.when(blk // 2 == p)
        def _():
            for h in range(3):
                send(*l0_kv(blk, h))

        for h in range(3):
            z = mm(sel(h), jnp.concatenate([KV[blk, h], QQ[blk, h]], axis=1)).astype(BF)
            ZKV1[h, blk] = z[0:128, :128]
            ZKV2[h, blk] = z[128:192, :128]
            ZKV3[h, blk] = z[192:224, :128]
            ZQ[h, blk] = z[:, 128:]
            send(*l1_kv(blk, h))

    def far_levels(blk):
        for h in range(3):
            send(*l2_kv(blk, h))
            send(*l3_kv(blk, h))

    def fwd(src_slot, dst_slot, sub, part, n, dev):
        c = rcopy(T.at[src_slot, rows_of(sub, part)], T.at[dst_slot, rows_of(sub, part)], ts.at[n], tr.at[n], dev)
        c.start()
        sends.append(c)

    def share(slot, sub, n):
        r = rows_of(sub, (0, 64))
        c = rcopy(T.at[slot, r], T.at[slot, r], cs.at[n], cr.at[n], n_core)
        c.start()
        sends.append(c)

    def landed(slot, sub, part, n):
        arrived(T.at[slot, rows_of(sub, part)], tr.at[n])

    def shared(slot, sub, n):
        arrived(T.at[slot, other_rows(sub)], cr.at[n])

    pl.semaphore_wait(sxa, 2)
    tell(sya, y_next)
    project(TOK, zh)
    pl.semaphore_wait(sya, 2)
    tell(sxb, x_next)

    for k, part in enumerate(FAR):
        landed(0, zl, part, k)
        fwd(0, 1, zl, part, 6 + k, n_in)
    for k, part in enumerate(NEAR):
        own(zl, part, 4 + k)
    share(0, zl, 0)
    for k, part in enumerate(FAR):
        landed(1, 1 - zl, part, 6 + k)
        fwd(1, 2, 1 - zl, part, 12 + k, n_out)
    share(1, 1 - zl, 2)
    for k, part in enumerate(NEAR):
        landed(0, 1 - zl, part, 4 + k)
        fwd(0, 1, 1 - zl, part, 10 + k, n_in)
    share(0, 1 - zl, 1)
    shared(0, zl, 0)
    shared(0, 1 - zl, 1)
    project(T.at[0], g_out)
    pl.semaphore_wait(sxb, 2)
    far_levels(zh)
    far_levels(g_out)
    for k, part in enumerate(FAR):
        landed(2, zl, part, 12 + k)
        fwd(2, 2, zl, part, 16 + k, n_in)
    share(2, zl, 4)
    for k, part in enumerate(NEAR):
        landed(1, zl, part, 10 + k)
    share(1, zl, 3)
    shared(1, 1 - zl, 2)
    shared(1, zl, 3)
    project(T.at[1], (zh - dz + 4) % 4)
    far_levels((zh - dz + 4) % 4)

    for h in range(3):
        PQ0[h] = jnp.where(low, QQ[2 * p, h], QQ[2 * p + 1, h])
        q = jnp.where(low, ZQ[h, 2 * p], ZQ[h, 2 * p + 1])
        PQ1[h] = q[:128]
        PQ2[h] = q[128:192]
        PQ3[h] = q[192:224]
        for a in queries(h):
            send(*a)

    def attend(Q, K, R, tiles):
        VX[...] = jnp.where(low, jnp.ones((), BF), K[...])

        @pl.loop(0, tiles)
        def _(i):
            r = pl.ds(pl.multiple_of(i * 512, 512), 512)
            q = Q[r]
            qa = jnp.where(low, q, jnp.zeros((), BF))
            qb = jnp.where(low, pltpu.roll(q.astype(F32), 64, 1).astype(BF), jnp.zeros((), BF))
            k = K[...]
            v = VX[...]

            sa, sb = nt(qa, k), nt(qb, k)
            ma = jnp.max(sa, axis=1, keepdims=True)
            mb = jnp.max(sb, axis=1, keepdims=True)
            ua = mm(jnp.exp2((sa - ma) * (SCALE * LOG2E)).astype(BF), v)
            ub = mm(jnp.exp2((sb - mb) * (SCALE * LOG2E)).astype(BF), v)
            ra = pltpu.roll(ua, 64, 1)
            rb = pltpu.roll(ub, 64, 1)
            tot = jnp.where(low, ua, rb)
            o = jnp.where(low, ra, ub) / tot
            ll = SCALE * jnp.where(low, ma, mb) + jnp.log(tot)
            hi = ll.astype(BF)
            left = ll - hi.astype(F32)
            mid = left.astype(BF)
            tail = (left - mid.astype(F32)).astype(BF)
            l64 = lane & 63
            piece = jnp.where(l64 == 0, hi, jnp.where(l64 == 1, mid, jnp.where(l64 == 2, tail, jnp.zeros((), BF))))
            R[r, 0:128] = o.astype(BF)
            R[r, 128:256] = piece

    def ret0(xs):
        return at(RA, xs * 256, 256), R0.at[x_of], rs.at[xs], rr0.at[x_of], seq_at(y, zh, xs)

    def ret1(xs):
        return at(RB, xs * 128, 128), R123.at[x_of, 0:128], rs.at[4 + xs], rr.at[x_of, 0], seq_at(y, zh, xs)

    def ret2(R, head, first):
        def one(si):
            dst = seq_at(y2 + si // 4, zh, si % 4)
            return at(R, si * 64, 64), R123.at[head, 128:192], rs.at[first + si], rr.at[head, 1], dst

        return one

    head_3 = jnp.where(x_of == 2, 2, y // 2)

    def ret3(si):
        dst = seq_at(si // 4, zh, si % 4)
        return at(RC, si * 32, 32), R123.at[head_3, 192:224], rs.at[12 + si], rr.at[head_3, 2], dst

    ret2b = ret2(RB, 2 * (y % 2), 4)
    ret2c = ret2(RC, 1, 12)
    is_l2c = (x_of == 3) & (y % 2 == 0)
    is_l3 = ((x_of == 3) & (y % 2 == 1)) | ((x_of == 2) & (y == 0))

    def do_all(n, f, act):
        @pl.loop(0, n)
        def _(k):
            act(*f(k))

    for k, part in enumerate(FAR):
        landed(2, 1 - zl, part, 16 + k)
    share(2, 1 - zl, 5)
    shared(2, zl, 4)
    shared(2, 1 - zl, 5)
    project(T.at[2], (zh + 2) % 4)
    far_levels((zh + 2) % 4)

    load_wout.wait()

    def w_rows(first_row, n):
        return WF.at[pl.ds(pl.multiple_of(first_row, 64), n)]

    w_core = rcopy(WF.at[own_w], WF.at[own_w], ws.at[0], wr.at[0], n_core)
    w_in = rcopy(w_rows(384 * hd, 192), w_rows(384 * hd, 192), ws.at[1], wr.at[1], n_in)
    w_out = rcopy(w_rows(384 * hd + 192, 192), w_rows(384 * hd + 192, 192), ws.at[2], wr.at[2], n_out)
    for c in (w_core, w_in, w_out):
        c.start()
        sends.append(c)

    @pl.when(x_of != 3)
    def _():
        arrived(KA, lr.at[0])
        arrived(QA, lr.at[1])
        attend(QA, KA, RA, 2)
        do_all(4, ret0, send)

    arrived(KB, lr.at[2])
    arrived(QB, lr.at[3])
    attend(QB, KB, RB, 1)

    @pl.when(x_of != 3)
    def _():
        do_all(4, ret1, send)

    @pl.when(x_of == 3)
    def _():
        do_all(8, ret2b, send)

    @pl.when(is_l2c | is_l3)
    def _():
        arrived(KC, lr.at[4])
        arrived(QC, lr.at[5])
        attend(QC, KC, RC, 1)

    @pl.when(is_l2c)
    def _():
        do_all(8, ret2c, send)

    @pl.when(is_l3)
    def _():
        do_all(16, ret3, send)

    hd_in = (1 - zl) * 2 + core
    arrived(w_rows(384 * hd_in, 192), wr.at[1])
    arrived(w_rows(384 * hd_in + 192, 192), wr.at[2])
    w_pass = rcopy(w_rows(384 * hd_in, 384), w_rows(384 * hd_in, 384), ws.at[3], wr.at[3], n_core)
    w_pass.start()
    sends.append(w_pass)

    R123[:, 224:256] = jnp.zeros((3, 32, 256), BF)
    ji = lax.broadcasted_iota(jnp.int32, (128, 128), 0)
    jo = lax.broadcasted_iota(jnp.int32, (128, 128), 1)
    spread = jnp.where((ji // 64 == jo // 64) & (ji % 64 < 3), 1.0, 0.0).astype(BF)
    row = lax.broadcasted_iota(jnp.int32, (ROWS, 128), 0)
    for h in (1, 0, 2):
        arrived(R0.at[h], rr0.at[h])
        arrived(R123.at[h, 0:128], rr.at[h, 0])
        arrived(R123.at[h, 128:192], rr.at[h, 1])
        arrived(R123.at[h, 192:224], rr.at[h, 2])
        r0 = R0[h]
        os = [r0[:, :128].astype(F32)]
        logs = [mm(r0[:, 128:], spread)]
        r = R123[h]
        for l, (lo_row, hi_row) in ((1, (0, 128)), (2, (128, 192)), (3, (192, 224))):
            sc = mm(sel_t(h, lo_row, hi_row), r)
            os.append(sc[:, :128])
            lg = mm(sc[:, 128:].astype(BF), spread)
            o_l = offs[l, 3 * par + h] & (2**l - 1)
            logs.append(jnp.where((row & (2**l - 1)) == o_l, lg, ABSENT))
        best = jnp.maximum(jnp.maximum(logs[0], logs[1]), jnp.maximum(logs[2], logs[3]))
        wts = [jnp.exp(v - best) for v in logs]
        den = wts[0] + wts[1] + wts[2] + wts[3]
        num = wts[0] * os[0] + wts[1] * os[1] + wts[2] * os[2] + wts[3] * os[3]
        a = num / den
        CA[h] = a
        CR[h] = pltpu.roll(a, 64, 1)

    slot = par * 4 + hd
    for b in range(2):
        LO, HI = (CA, CR) if b == 0 else (CR, CA)
        two = jnp.where(low, LO[par], HI[par + 1])
        lo1, hi1 = LO[2 - 2 * par], HI[2 - 2 * par]
        for i in range(4):
            r = i * 64
            MS[b, i, 0:64] = two[r:r + 64].astype(BF)
            MS[b, i, 64:96] = jnp.where(low, lo1[r:r + 32], hi1[r + 32:r + 64]).astype(BF)

    def final(b, i):
        return MS.at[b, i], AT.at[slot], fs.at[b * 4 + i], fr.at[slot], seq_at(y, 2 * p + b, x), i

    @pl.loop(0, 8)
    def _(n):
        src, dst, ssem, rsem, dseq, dhd = final(n // 4, n % 4)

        @pl.when((dseq != sq) | (dhd != hd))
        def _():
            rcopy(src, dst, ssem, rsem, (dseq, dhd)).start()

        @pl.when((dseq == sq) & (dhd == hd))
        def _():
            pltpu.make_async_copy(src, dst, rsem).start()

    arrived(WF.at[pl.ds(pl.multiple_of(384 * (hd + 1 - 2 * core), 128), 384)], wr.at[0])
    arrived(WF.at[pl.ds(pl.multiple_of(384 * (hd_in + 1 - 2 * core), 128), 384)], wr.at[3])

    for i in range(4):
        arrived(AT.at[i], fr.at[i])
        arrived(AT.at[4 + i], fr.at[4 + i])
        e, o = AT[i], AT[4 + i]
        x0 = e[64:96].astype(F32)
        x1 = o[64:96].astype(F32)
        AF[:, i * 384:i * 384 + 128] = e[:64]
        AF[0:32, i * 384 + 128:i * 384 + 256] = jnp.where(low, x0, pltpu.roll(x1, 64, 1)).astype(BF)
        AF[32:64, i * 384 + 128:i * 384 + 256] = jnp.where(low, pltpu.roll(x0, 64, 1), x1).astype(BF)
        AF[:, i * 384 + 256:(i + 1) * 384] = o[:64]
    out[...] = mm(AF[...], WF[...]).astype(BF)

    for c in sends:
        c.wait_send()

    @pl.loop(0, 8)
    def _(n):
        src, dst, ssem, rsem, dseq, dhd = final(n // 4, n % 4)

        @pl.when((dseq != sq) | (dhd != hd))
        def _():
            rcopy(src, dst, ssem, rsem, (dseq, dhd)).wait_send()

    for h in range(3):
        for b in range(2):
            sent(*l0_kv(2 * p + b, h))
        for a in queries(h):
            sent(*a)

    @pl.loop(0, 4)
    def _(blk):
        for h in range(3):
            sent(*l1_kv(blk, h))
            sent(*l2_kv(blk, h))
            sent(*l3_kv(blk, h))

    @pl.when(x_of != 3)
    def _():
        do_all(4, ret0, sent)
        do_all(4, ret1, sent)

    @pl.when(x_of == 3)
    def _():
        do_all(8, ret2b, sent)

    @pl.when(is_l2c)
    def _():
        do_all(8, ret2c, sent)

    @pl.when(is_l3)
    def _():
        do_all(16, ret3, sent)


def local(tokens, query_weight, key_weight, value_weight, offsets, out_weight):
    vm = lambda *s: pltpu.VMEM(s, BF)
    dma = lambda *s: pltpu.SemaphoreType.DMA(s)
    return pl.pallas_call(
        body,
        out_shape=jax.ShapeDtypeStruct((64, D), BF),
        in_specs=[pl.BlockSpec(memory_space=pl.ANY)] * 5 + [pl.BlockSpec(memory_space=pltpu.SMEM)],
        out_specs=pl.BlockSpec(memory_space=pltpu.VMEM),
        scratch_shapes=[
            vm(256, D), vm(3, D, 256), vm(3, D, 256), vm(D, D),
            vm(3, 256, D), vm(4, 3, 256, 128), vm(4, 3, 256, 128),
            vm(3, 4, 128, 128), vm(3, 4, 64, 128), vm(3, 4, 32, 128), vm(3, 4, 256, 128),
            vm(3, 256, 128), vm(3, 128, 128), vm(3, 64, 128), vm(3, 32, 128),
            vm(2048, 128), vm(1024, 128), vm(2048, 128), vm(512, 128), vm(2048, 128), vm(512, 128), vm(2048, 128),
            vm(1024, 256), vm(512, 256), vm(512, 256), vm(3, 256, 256), vm(3, 256, 256),
            pltpu.VMEM((3, 256, 128), F32), pltpu.VMEM((3, 256, 128), F32),
            vm(2, 4, 96, 128), vm(8, 96, 128), vm(64, D),
            dma(5), dma(20), dma(20), dma(6), dma(6), dma(15, 4), dma(6), dma(28), dma(3), dma(3, 3),
            dma(4), dma(4), dma(8), dma(8),
            pltpu.SemaphoreType.REGULAR, pltpu.SemaphoreType.REGULAR, pltpu.SemaphoreType.REGULAR,
        ],
        compiler_params=pltpu.CompilerParams(
            has_side_effects=True, collective_id=1, vmem_limit_bytes=62 * 1024 * 1024
        ),
    )(tokens, query_weight, key_weight, value_weight, out_weight, offsets)


def solution(mesh):
    return jax.shard_map(
        local,
        mesh=mesh,
        in_specs=(
            P("seq", None),
            P(None, "head"),
            P(None, "head"),
            P(None, "head"),
            P(None, "head"),
            P("head", None),
        ),
        out_specs=P(("seq", "head"), None),
        check_vma=False,
    )
```

```python
import jax
import jax.numpy as jnp
from jax import lax
from jax.experimental import pallas as pl
from jax.experimental.pallas import tpu as pltpu
from jax.sharding import PartitionSpec as P

MESH = pl.DeviceIdType.MESH
BF = jnp.bfloat16
F32 = jnp.float32
ROWS = 256
D = 1536
HALF = 128
SCALE = 0.125
LOG2E = 1.4426950408889634
ABSENT = -1e30


def nt(a, b):
    return lax.dot_general(a, b, (((1,), (1,)), ((), ())), preferred_element_type=F32)


def mm(a, b):
    return jnp.dot(a, b, preferred_element_type=F32)


def body(
    tok, wq, wk, wv, wout, offs, out,
    TOK, WIN, W3, WF, T, KV, ZKV1, ZKV2, ZKV3, PQ0, PQ1, PQ2, PQ3,
    K, Q, VX, R, R0, R123, CA, CR, MS, AT, AF,
    win, ts, tr, cs, cr, ls, lr, rs, rr0, rr, ws, wr, fs, fr,
    sxa, sya, sxb,
):
    sq = lax.axis_index("seq")
    hd = lax.axis_index("head")
    y = sq // 16
    zh = (sq // 4) % 4
    x = sq % 4
    zl = hd // 2
    core = hd % 2
    par = zh % 2
    p = zh // 2

    def seq_at(yy, zz, xx):
        return yy * 16 + zz * 4 + xx

    dz = 2 * zl - 1
    g_out = (zh + dz + 4) % 4
    n_out = (seq_at(y, g_out, x), (1 - zl) * 2 + core)
    n_in = (sq, (1 - zl) * 2 + core)
    n_core = (sq, zl * 2 + (1 - core))

    barrier = pltpu.get_barrier_semaphore()

    def hello(dev):
        pl.semaphore_signal(barrier, inc=1, device_id=dev, device_id_type=MESH)

    hello(n_out)
    hello(n_in)
    hello(n_core)
    x_next = [(seq_at(y, zh, (x + d) % 4), hd) for d in (1, 3)]
    y_next = [(seq_at((y + d) % 4, zh, x), hd) for d in (1, 3)]
    for dev in x_next + y_next:
        hello(dev)

    def tell(sem, devs):
        for dev in devs:
            pl.semaphore_signal(sem, inc=1, device_id=dev, device_id_type=MESH)

    start = pl.multiple_of(128 * par, 128)
    loads = [pltpu.make_async_copy(wsrc.at[:, pl.ds(start, 256)], WIN.at[n], win.at[n]) for n, wsrc in enumerate((wk, wv, wq))]
    own_w = pl.ds(pl.multiple_of(384 * hd, 128), 384)
    load_tok = pltpu.make_async_copy(tok, TOK, win.at[3])
    load_wout = pltpu.make_async_copy(wout, WF.at[own_w], win.at[4])
    load_tok.start()
    for c in loads:
        c.start()
    load_wout.start()

    def rcopy(src, dst, ssem, rsem, dev):
        return pltpu.make_async_remote_copy(
            src_ref=src, dst_ref=dst, send_sem=ssem, recv_sem=rsem, device_id=dev, device_id_type=MESH
        )

    def send(src, dst, ssem, rsem, dst_seq):
        @pl.when(dst_seq != sq)
        def _():
            rcopy(src, dst, ssem, rsem, (dst_seq, hd)).start()

        @pl.when(dst_seq == sq)
        def _():
            pltpu.make_async_copy(src, dst, rsem).start()

    def sent(src, dst, ssem, rsem, dst_seq):
        @pl.when(dst_seq != sq)
        def _():
            rcopy(src, dst, ssem, rsem, (dst_seq, hd)).wait_send()

    def arrived(ref, sem):
        pltpu.make_async_copy(ref, ref, sem).wait()

    lane = lax.broadcasted_iota(jnp.int32, (1, 128), 1)
    low = lane < 64

    lo = core * HALF

    FAR = [(i * 16, 16) for i in range(4)]
    NEAR = [(i * 32, 32) for i in range(2)]

    def rows_of(sub, part):
        return pl.ds(pl.multiple_of(lo + sub * 64 + part[0], part[1]), part[1])

    def other_rows(sub):
        return pl.ds(pl.multiple_of(HALF - lo + sub * 64, 64), 64)

    load_tok.wait()
    pl.semaphore_wait(barrier, 7)
    sends = []

    def own(sub, part, n):
        c = rcopy(TOK.at[rows_of(sub, part)], T.at[0, rows_of(sub, part)], ts.at[n], tr.at[n], n_out)
        c.start()
        sends.append(c)

    for k, part in enumerate(FAR):
        own(1 - zl, part, k)
    for k, part in enumerate(NEAR):
        own(zl, part, 4 + k)

    tell(sxa, x_next)

    for c in loads:
        c.wait()

    def mover(rows, with_part):
        r = lax.broadcasted_iota(jnp.int32, (rows, 384), 0)
        c = lax.broadcasted_iota(jnp.int32, (rows, 384), 1)
        src = 64 * par + (c // 128) * 64 + c % 64
        if with_part:
            src = src + ((c // 64) % 2) * 256
        return jnp.where(r == src, 1.0, 0.0).astype(BF)

    pkv = mover(512, True)
    pq = mover(256, False)

    @pl.loop(0, 6)
    def _(i):
        r = pl.ds(pl.multiple_of(i * 256, 256), 256)
        wkv = mm(WIN[0, r], pkv[:256]) + mm(WIN[1, r], pkv[256:])
        wqq = mm(WIN[2, r], pq)
        for h in range(3):
            W3[h, r, 0:128] = wkv[:, h * 128:(h + 1) * 128].astype(BF)
            W3[h, r, 128:256] = wqq[:, h * 128:(h + 1) * 128].astype(BF)

    def targets(h, i):
        o1 = offs[1, 3 * par + h] & 1
        o2 = offs[2, 3 * par + h] & 3
        o3 = offs[3, 3 * par + h] & 7
        t1 = i * 2 + o1
        t2 = (i - 128) * 4 + o2
        t3 = (i - 192) * 8 + o3
        return jnp.where(i < 128, t1, jnp.where(i < 192, t2, jnp.where(i < 224, t3, -1)))

    def sel(h):
        i = lax.broadcasted_iota(jnp.int32, (ROWS, ROWS), 0)
        c = lax.broadcasted_iota(jnp.int32, (ROWS, ROWS), 1)
        return jnp.where(targets(h, i) == c, 1.0, 0.0).astype(BF)

    def sel_t(h, first_row, last_row):
        i = lax.broadcasted_iota(jnp.int32, (ROWS, ROWS), 1)
        c = lax.broadcasted_iota(jnp.int32, (ROWS, ROWS), 0)
        level = {0: 1, 128: 2, 192: 3}[first_row]
        n = (last_row - first_row) // 2
        j = i - first_row
        o = offs[level, 3 * par + h] & (2**level - 1)
        hit = ((j // n) * 128 + (j % n) * 2**level + o == c) & (i >= first_row) & (i < last_row)
        return jnp.where(hit, 1.0, 0.0).astype(BF)

    def role_seq(role, yy):
        return seq_at(yy, zh, (role + 2 * core) % 4)

    x_of = (x + 2 * core) % 4

    def at(ref, first_row, n):
        return ref.at[pl.ds(pl.multiple_of(first_row, n), n)]

    s2 = (y % 2) * 4 + x
    s3 = y * 4 + x
    y2 = y - y % 2

    L2_AT = ((3, 0, 1), (3, 0, 2), (3, 1, 1))
    L3_AT = ((3, 1), (3, 3), (2, 0))

    def l0_kv(blk, h):
        b = blk % 2
        return KV.at[blk, h], at(K.at[0], x * 512 + b * 256, 256), ls.at[h, b], lr.at[0], role_seq(h, y)

    def l1_kv(blk, h):
        return ZKV1.at[h, blk], at(K.at[1], x * 512 + blk * 128, 128), ls.at[3 + h, blk], lr.at[2], role_seq(h, y)

    def l2_kv(blk, h):
        role, dy, c = L2_AT[h]
        dst = at(K.at[c], s2 * 256 + blk * 64, 64)
        return ZKV2.at[h, blk], dst, ls.at[6 + h, blk], lr.at[2 * c], role_seq(role, y2 + dy)

    def l3_kv(blk, h):
        role, yy = L3_AT[h]
        return ZKV3.at[h, blk], at(K.at[2], s3 * 128 + blk * 32, 32), ls.at[9 + h, blk], lr.at[4], role_seq(role, yy)

    def near_queries(blk, h):
        b = blk % 2
        return [
            (PQ0.at[h, b], at(Q.at[x // 2], (x % 2) * 256 + b * 128, 128), ls.at[12 + h, b], lr.at[1], role_seq(h, y)),
            (PQ1.at[h, b], at(Q.at[2], x * 128 + b * 64, 64), ls.at[12 + h, 2 + b], lr.at[3], role_seq(h, y)),
        ]

    def far_queries(blk, h):
        b = blk % 2
        r2, dy, c = L2_AT[h]
        r3, yy = L3_AT[h]
        dst = at(Q.at[c + 1], s2 * 64 + b * 32, 32)
        return [
            (PQ2.at[h, b], dst, ls.at[15 + h, b], lr.at[2 * c + 1], role_seq(r2, y2 + dy)),
            (PQ3.at[h, b], at(Q.at[3], s3 * 32 + b * 16, 16), ls.at[15 + h, 2 + b], lr.at[5], role_seq(r3, yy)),
        ]

    def project_head(xs, blk, h):
        own_pair = blk // 2 == p
        yh = mm(xs, W3[h]).astype(BF)
        KV[blk, h] = yh[:, :128]

        @pl.when(own_pair)
        def _():
            PQ0[h, blk % 2] = jnp.where(low, yh[:128, 128:], yh[128:, 128:])
            send(*l0_kv(blk, h))

        z = mm(sel(h), yh).astype(BF)
        ZKV1[h, blk] = z[0:128, :128]
        ZKV2[h, blk] = z[128:192, :128]
        ZKV3[h, blk] = z[192:224, :128]
        send(*l1_kv(blk, h))

        @pl.when(own_pair)
        def _():
            b = blk % 2
            PQ1[h, b] = jnp.where(low, z[0:64, 128:], z[64:128, 128:])
            PQ2[h, b] = jnp.where(low, z[128:160, 128:], z[160:192, 128:])
            PQ3[h, b] = jnp.where(low, z[192:208, 128:], z[208:224, 128:])
            for a in near_queries(blk, h):
                send(*a)

    def project(x_ref, blk):
        xs = x_ref[...]
        for h in range(3):
            project_head(xs, blk, h)

    def far_levels(blk):
        for h in range(3):
            send(*l2_kv(blk, h))
            send(*l3_kv(blk, h))

        @pl.when(blk // 2 == p)
        def _():
            for h in range(3):
                for a in far_queries(blk, h):
                    send(*a)

    def fwd(src_slot, dst_slot, sub, part, n, dev):
        c = rcopy(T.at[src_slot, rows_of(sub, part)], T.at[dst_slot, rows_of(sub, part)], ts.at[n], tr.at[n], dev)
        c.start()
        sends.append(c)

    def share(slot, sub, n):
        r = rows_of(sub, (0, 64))
        c = rcopy(T.at[slot, r], T.at[slot, r], cs.at[n], cr.at[n], n_core)
        c.start()
        sends.append(c)

    def landed(slot, sub, part, n):
        arrived(T.at[slot, rows_of(sub, part)], tr.at[n])

    def shared(slot, sub, n):
        arrived(T.at[slot, other_rows(sub)], cr.at[n])

    for k, part in enumerate(FAR):
        landed(0, zl, part, k)
        fwd(0, 1, zl, part, 6 + k, n_in)
    share(0, zl, 0)
    pl.semaphore_wait(sxa, 2)
    tell(sya, y_next)
    project(TOK, zh)
    pl.semaphore_wait(sya, 2)
    tell(sxb, x_next)
    for k, part in enumerate(NEAR):
        landed(0, 1 - zl, part, 4 + k)
        fwd(0, 1, 1 - zl, part, 10 + k, n_in)
    share(0, 1 - zl, 1)
    for k, part in enumerate(FAR):
        landed(1, 1 - zl, part, 6 + k)
        fwd(1, 2, 1 - zl, part, 12 + k, n_out)
    share(1, 1 - zl, 2)
    pl.semaphore_wait(sxb, 2)
    far_levels(zh)
    shared(0, zl, 0)
    shared(0, 1 - zl, 1)
    for k, part in enumerate(FAR):
        if k < 3:
            project_head(T[0], g_out, k)
        landed(2, zl, part, 12 + k)
        fwd(2, 2, zl, part, 16 + k, n_in)
    share(2, zl, 4)
    far_levels(g_out)
    for k, part in enumerate(NEAR):
        landed(1, zl, part, 10 + k)
    share(1, zl, 3)
    shared(1, 1 - zl, 2)
    shared(1, zl, 3)
    project(T.at[1], (zh - dz + 4) % 4)
    far_levels((zh - dz + 4) % 4)

    def attend(t):
        job = jnp.maximum(t - 1, 0)
        VX[...] = jnp.where(low, jnp.ones((), BF), K[job])
        q = Q[t]
        qa = jnp.where(low, q, jnp.zeros((), BF))
        qb = jnp.where(low, pltpu.roll(q.astype(F32), 64, 1).astype(BF), jnp.zeros((), BF))
        k = K[job]
        v = VX[...]

        sa, sb = nt(qa, k), nt(qb, k)
        ma = jnp.max(sa, axis=1, keepdims=True)
        mb = jnp.max(sb, axis=1, keepdims=True)
        ua = mm(jnp.exp2((sa - ma) * (SCALE * LOG2E)).astype(BF), v)
        ub = mm(jnp.exp2((sb - mb) * (SCALE * LOG2E)).astype(BF), v)
        ra = pltpu.roll(ua, 64, 1)
        rb = pltpu.roll(ub, 64, 1)
        tot = jnp.where(low, ua, rb)
        o = jnp.where(low, ra, ub) / tot
        ll = SCALE * jnp.where(low, ma, mb) + jnp.log(tot)
        hi = ll.astype(BF)
        left = ll - hi.astype(F32)
        mid = left.astype(BF)
        tail = (left - mid.astype(F32)).astype(BF)
        l64 = lane & 63
        piece = jnp.where(l64 == 0, hi, jnp.where(l64 == 1, mid, jnp.where(l64 == 2, tail, jnp.zeros((), BF))))
        R[t, :, 0:128] = o.astype(BF)
        R[t, :, 128:256] = piece

    def ret0(xs):
        src = at(R.at[xs // 2], (xs % 2) * 256, 256)
        return src, R0.at[x_of], rs.at[xs], rr0.at[x_of], seq_at(y, zh, xs)

    def ret1(xs):
        return at(R.at[2], xs * 128, 128), R123.at[x_of, 0:128], rs.at[4 + xs], rr.at[x_of, 0], seq_at(y, zh, xs)

    def ret2(tile, head, first):
        def one(si):
            dst = seq_at(y2 + si // 4, zh, si % 4)
            return at(R.at[tile], si * 64, 64), R123.at[head, 128:192], rs.at[first + si], rr.at[head, 1], dst

        return one

    head_3 = jnp.where(x_of == 2, 2, y // 2)

    def ret3(si):
        dst = seq_at(si // 4, zh, si % 4)
        return at(R.at[3], si * 32, 32), R123.at[head_3, 192:224], rs.at[12 + si], rr.at[head_3, 2], dst

    ret2b = ret2(2, 2 * (y % 2), 4)
    ret2c = ret2(3, 1, 12)
    is_l2c = (x_of == 3) & (y % 2 == 0)
    is_l3 = ((x_of == 3) & (y % 2 == 1)) | ((x_of == 2) & (y == 0))

    def do_all(n, f, act):
        @pl.loop(0, n)
        def _(k):
            act(*f(k))

    for k, part in enumerate(FAR):
        landed(2, 1 - zl, part, 16 + k)
    share(2, 1 - zl, 5)
    shared(2, zl, 4)
    shared(2, 1 - zl, 5)
    project(T.at[2], (zh + 2) % 4)
    far_levels((zh + 2) % 4)

    load_wout.wait()

    def w_rows(first_row, n):
        return WF.at[pl.ds(pl.multiple_of(first_row, 64), n)]

    w_core = rcopy(WF.at[own_w], WF.at[own_w], ws.at[0], wr.at[0], n_core)
    w_in = rcopy(w_rows(384 * hd, 192), w_rows(384 * hd, 192), ws.at[1], wr.at[1], n_in)
    w_out = rcopy(w_rows(384 * hd + 192, 192), w_rows(384 * hd + 192, 192), ws.at[2], wr.at[2], n_out)
    for c in (w_core, w_in, w_out):
        c.start()
        sends.append(c)

    first = jnp.where(x_of == 3, 2, 0)
    last = jnp.where(is_l2c | is_l3, 4, 3)

    @pl.loop(first, last)
    def _(t):
        for n, first_tile in enumerate((0, 2, 3)):

            @pl.when(t == first_tile)
            def _():
                arrived(K.at[n], lr.at[2 * n])
                if n == 0:
                    arrived(Q.at[0:2], lr.at[1])
                else:
                    arrived(Q.at[n + 1], lr.at[2 * n + 1])

        attend(t)

        @pl.when(t < 2)
        def _():
            send(*ret0(2 * t))
            send(*ret0(2 * t + 1))

        @pl.when((t == 2) & (x_of != 3))
        def _():
            do_all(4, ret1, send)

        @pl.when((t == 2) & (x_of == 3))
        def _():
            do_all(8, ret2b, send)

        @pl.when((t == 3) & is_l2c)
        def _():
            do_all(8, ret2c, send)

        @pl.when((t == 3) & is_l3)
        def _():
            do_all(16, ret3, send)

    hd_in = (1 - zl) * 2 + core
    arrived(w_rows(384 * hd_in, 192), wr.at[1])
    arrived(w_rows(384 * hd_in + 192, 192), wr.at[2])
    w_pass = rcopy(w_rows(384 * hd_in, 384), w_rows(384 * hd_in, 384), ws.at[3], wr.at[3], n_core)
    w_pass.start()
    sends.append(w_pass)

    R123[:, 224:256] = jnp.zeros((3, 32, 256), BF)
    ji = lax.broadcasted_iota(jnp.int32, (128, 128), 0)
    jo = lax.broadcasted_iota(jnp.int32, (128, 128), 1)
    spread = jnp.where((ji // 64 == jo // 64) & (ji % 64 < 3), 1.0, 0.0).astype(BF)
    row = lax.broadcasted_iota(jnp.int32, (ROWS, 128), 0)
    for h in (1, 0, 2):
        arrived(R0.at[h], rr0.at[h])
        arrived(R123.at[h, 0:128], rr.at[h, 0])
        arrived(R123.at[h, 128:192], rr.at[h, 1])
        arrived(R123.at[h, 192:224], rr.at[h, 2])
        r0 = R0[h]
        os = [r0[:, :128].astype(F32)]
        logs = [mm(r0[:, 128:], spread)]
        r = R123[h]
        for l, (lo_row, hi_row) in ((1, (0, 128)), (2, (128, 192)), (3, (192, 224))):
            sc = mm(sel_t(h, lo_row, hi_row), r)
            os.append(sc[:, :128])
            lg = mm(sc[:, 128:].astype(BF), spread)
            o_l = offs[l, 3 * par + h] & (2**l - 1)
            logs.append(jnp.where((row & (2**l - 1)) == o_l, lg, ABSENT))
        best = jnp.maximum(jnp.maximum(logs[0], logs[1]), jnp.maximum(logs[2], logs[3]))
        wts = [jnp.exp(v - best) for v in logs]
        den = wts[0] + wts[1] + wts[2] + wts[3]
        num = wts[0] * os[0] + wts[1] * os[1] + wts[2] * os[2] + wts[3] * os[3]
        a = num / den
        CA[h] = a
        CR[h] = pltpu.roll(a, 64, 1)

    slot = par * 4 + hd
    for i in range(4):
        LO, HI = (CA, CR) if i < 2 else (CR, CA)
        two = jnp.where(low, LO[par], HI[par + 1])
        lo1, hi1 = LO[2 - 2 * par], HI[2 - 2 * par]
        for b in range(2):
            r = b * 128 + (i % 2) * 64
            MS[b, i, 0:64] = two[r:r + 64].astype(BF)
            MS[b, i, 64:96] = jnp.where(low, lo1[r:r + 32], hi1[r + 32:r + 64]).astype(BF)

    def final(b, i):
        return MS.at[b, i], AT.at[slot], fs.at[b * 4 + i], fr.at[slot], seq_at(y, 2 * p + b, x), i

    @pl.loop(0, 8)
    def _(n):
        src, dst, ssem, rsem, dseq, dhd = final(n // 4, n % 4)

        @pl.when((dseq != sq) | (dhd != hd))
        def _():
            rcopy(src, dst, ssem, rsem, (dseq, dhd)).start()

        @pl.when((dseq == sq) & (dhd == hd))
        def _():
            pltpu.make_async_copy(src, dst, rsem).start()

    arrived(WF.at[pl.ds(pl.multiple_of(384 * (hd + 1 - 2 * core), 128), 384)], wr.at[0])
    arrived(WF.at[pl.ds(pl.multiple_of(384 * (hd_in + 1 - 2 * core), 128), 384)], wr.at[3])

    for i in range(4):
        arrived(AT.at[i], fr.at[i])
        arrived(AT.at[4 + i], fr.at[4 + i])
        e, o = AT[i], AT[4 + i]
        x0 = e[64:96].astype(F32)
        x1 = o[64:96].astype(F32)
        AF[:, i * 384:i * 384 + 128] = e[:64]
        AF[0:32, i * 384 + 128:i * 384 + 256] = jnp.where(low, x0, pltpu.roll(x1, 64, 1)).astype(BF)
        AF[32:64, i * 384 + 128:i * 384 + 256] = jnp.where(low, pltpu.roll(x0, 64, 1), x1).astype(BF)
        AF[:, i * 384 + 256:(i + 1) * 384] = o[:64]
    out[...] = mm(AF[...], WF[...]).astype(BF)

    for c in sends:
        c.wait_send()

    @pl.loop(0, 8)
    def _(n):
        src, dst, ssem, rsem, dseq, dhd = final(n // 4, n % 4)

        @pl.when((dseq != sq) | (dhd != hd))
        def _():
            rcopy(src, dst, ssem, rsem, (dseq, dhd)).wait_send()

    for h in range(3):
        for b in range(2):
            sent(*l0_kv(2 * p + b, h))
            for a in near_queries(2 * p + b, h) + far_queries(2 * p + b, h):
                sent(*a)

    @pl.loop(0, 4)
    def _(blk):
        for h in range(3):
            sent(*l1_kv(blk, h))
            sent(*l2_kv(blk, h))
            sent(*l3_kv(blk, h))

    @pl.when(x_of != 3)
    def _():
        do_all(4, ret0, sent)
        do_all(4, ret1, sent)

    @pl.when(x_of == 3)
    def _():
        do_all(8, ret2b, sent)

    @pl.when(is_l2c)
    def _():
        do_all(8, ret2c, sent)

    @pl.when(is_l3)
    def _():
        do_all(16, ret3, sent)


def local(tokens, query_weight, key_weight, value_weight, offsets, out_weight):
    vm = lambda *s: pltpu.VMEM(s, BF)
    dma = lambda *s: pltpu.SemaphoreType.DMA(s)
    return pl.pallas_call(
        body,
        out_shape=jax.ShapeDtypeStruct((64, D), BF),
        in_specs=[pl.BlockSpec(memory_space=pl.ANY)] * 5 + [pl.BlockSpec(memory_space=pltpu.SMEM)],
        out_specs=pl.BlockSpec(memory_space=pltpu.VMEM),
        scratch_shapes=[
            vm(256, D), vm(3, D, 256), vm(3, D, 256), vm(D, D),
            vm(3, 256, D), vm(4, 3, 256, 128),
            vm(3, 4, 128, 128), vm(3, 4, 64, 128), vm(3, 4, 32, 128),
            vm(3, 2, 128, 128), vm(3, 2, 64, 128), vm(3, 2, 32, 128), vm(3, 2, 16, 128),
            vm(3, 2048, 128), vm(4, 512, 128), vm(2048, 128), vm(4, 512, 256), vm(3, 256, 256), vm(3, 256, 256),
            pltpu.VMEM((3, 256, 128), F32), pltpu.VMEM((3, 256, 128), F32),
            vm(2, 4, 96, 128), vm(8, 96, 128), vm(64, D),
            dma(5), dma(20), dma(20), dma(6), dma(6), dma(18, 4), dma(6), dma(28), dma(3), dma(3, 3),
            dma(4), dma(4), dma(8), dma(8),
            pltpu.SemaphoreType.REGULAR, pltpu.SemaphoreType.REGULAR, pltpu.SemaphoreType.REGULAR,
        ],
        compiler_params=pltpu.CompilerParams(
            has_side_effects=True, collective_id=1, vmem_limit_bytes=62 * 1024 * 1024
        ),
    )(tokens, query_weight, key_weight, value_weight, out_weight, offsets)


def solution(mesh):
    return jax.shard_map(
        local,
        mesh=mesh,
        in_specs=(
            P("seq", None),
            P(None, "head"),
            P(None, "head"),
            P(None, "head"),
            P(None, "head"),
            P("head", None),
        ),
        out_specs=P(("seq", "head"), None),
        check_vma=False,
    )
```

```python
import jax
import jax.numpy as jnp
from jax import lax
from jax.experimental import pallas as pl
from jax.experimental.pallas import tpu as pltpu
from jax.sharding import PartitionSpec as P

MESH = pl.DeviceIdType.MESH
BF = jnp.bfloat16
F32 = jnp.float32
ROWS = 256
D = 1536
HALF = 128
SCALE = 0.125
LOG2E = 1.4426950408889634
ABSENT = -1e30


def nt(a, b):
    return lax.dot_general(a, b, (((1,), (1,)), ((), ())), preferred_element_type=F32)


def mm(a, b):
    return jnp.dot(a, b, preferred_element_type=F32)


def body(
    tok, wq, wk, wv, wout, offs, out,
    TOK, WIN, W3, WF, T, KV, ZKV1, ZKV2, ZKV3, PQ0, PQ1, PQ2, PQ3,
    K, Q, VX, R, R0, R123, CA, CR, MS, AT, AF,
    win, ts, tr, cs, cr, ls, lr, rs, rr0, rr, ws, wr, fs, fr,
    sxa, sya, sxb,
):
    sq = lax.axis_index("seq")
    hd = lax.axis_index("head")
    y = sq // 16
    zh = (sq // 4) % 4
    x = sq % 4
    zl = hd // 2
    core = hd % 2
    par = zh % 2
    p = zh // 2

    def seq_at(yy, zz, xx):
        return yy * 16 + zz * 4 + xx

    dz = 2 * zl - 1
    g_out = (zh + dz + 4) % 4
    n_out = (seq_at(y, g_out, x), (1 - zl) * 2 + core)
    n_in = (sq, (1 - zl) * 2 + core)
    n_core = (sq, zl * 2 + (1 - core))

    barrier = pltpu.get_barrier_semaphore()

    def hello(dev):
        pl.semaphore_signal(barrier, inc=1, device_id=dev, device_id_type=MESH)

    hello(n_out)
    hello(n_in)
    hello(n_core)
    x_next = [(seq_at(y, zh, (x + d) % 4), hd) for d in (1, 3)]
    y_next = [(seq_at((y + d) % 4, zh, x), hd) for d in (1, 3)]
    for dev in x_next + y_next:
        hello(dev)

    def tell(sem, devs):
        for dev in devs:
            pl.semaphore_signal(sem, inc=1, device_id=dev, device_id_type=MESH)

    start = pl.multiple_of(128 * par, 128)
    loads = [pltpu.make_async_copy(wsrc.at[:, pl.ds(start, 256)], WIN.at[n], win.at[n]) for n, wsrc in enumerate((wk, wv, wq))]
    own_w = pl.ds(pl.multiple_of(384 * hd, 128), 384)
    load_tok = pltpu.make_async_copy(tok, TOK, win.at[3])
    load_wout = pltpu.make_async_copy(wout, WF.at[own_w], win.at[4])
    for c in loads:
        c.start()
    load_tok.start()

    def rcopy(src, dst, ssem, rsem, dev):
        return pltpu.make_async_remote_copy(
            src_ref=src, dst_ref=dst, send_sem=ssem, recv_sem=rsem, device_id=dev, device_id_type=MESH
        )

    def send(src, dst, ssem, rsem, dst_seq):
        @pl.when(dst_seq != sq)
        def _():
            rcopy(src, dst, ssem, rsem, (dst_seq, hd)).start()

        @pl.when(dst_seq == sq)
        def _():
            pltpu.make_async_copy(src, dst, rsem).start()

    def sent(src, dst, ssem, rsem, dst_seq):
        @pl.when(dst_seq != sq)
        def _():
            rcopy(src, dst, ssem, rsem, (dst_seq, hd)).wait_send()

    def arrived(ref, sem):
        pltpu.make_async_copy(ref, ref, sem).wait()

    lane = lax.broadcasted_iota(jnp.int32, (1, 128), 1)
    low = lane < 64

    lo = core * HALF

    FAR = [(i * 16, 16) for i in range(4)]
    NEAR = [(i * 32, 32) for i in range(2)]

    def rows_of(sub, part):
        return pl.ds(pl.multiple_of(lo + sub * 64 + part[0], part[1]), part[1])

    def other_rows(sub):
        return pl.ds(pl.multiple_of(HALF - lo + sub * 64, 64), 64)

    pl.semaphore_wait(barrier, 7)
    sends = []

    def own(sub, part, n):
        c = rcopy(tok.at[rows_of(sub, part)], T.at[0, rows_of(sub, part)], ts.at[n], tr.at[n], n_out)
        c.start()
        sends.append(c)

    for k, part in enumerate(FAR):
        own(1 - zl, part, k)
    for k, part in enumerate(NEAR):
        own(zl, part, 4 + k)

    tell(sxa, x_next)

    for c in loads:
        c.wait()
    load_tok.wait()

    def mover(rows, with_part):
        r = lax.broadcasted_iota(jnp.int32, (rows, 384), 0)
        c = lax.broadcasted_iota(jnp.int32, (rows, 384), 1)
        src = 64 * par + (c // 128) * 64 + c % 64
        if with_part:
            src = src + ((c // 64) % 2) * 256
        return jnp.where(r == src, 1.0, 0.0).astype(BF)

    pkv = mover(512, True)
    pq = mover(256, False)

    @pl.loop(0, 6)
    def _(i):
        r = pl.ds(pl.multiple_of(i * 256, 256), 256)
        wkv = mm(WIN[0, r], pkv[:256]) + mm(WIN[1, r], pkv[256:])
        wqq = mm(WIN[2, r], pq)
        for h in range(3):
            W3[h, r, 0:128] = wkv[:, h * 128:(h + 1) * 128].astype(BF)
            W3[h, r, 128:256] = wqq[:, h * 128:(h + 1) * 128].astype(BF)

    load_wout.start()

    def targets(h, i):
        o1 = offs[1, 3 * par + h] & 1
        o2 = offs[2, 3 * par + h] & 3
        o3 = offs[3, 3 * par + h] & 7
        t1 = i * 2 + o1
        t2 = (i - 128) * 4 + o2
        t3 = (i - 192) * 8 + o3
        return jnp.where(i < 128, t1, jnp.where(i < 192, t2, jnp.where(i < 224, t3, -1)))

    def sel(h):
        i = lax.broadcasted_iota(jnp.int32, (ROWS, ROWS), 0)
        c = lax.broadcasted_iota(jnp.int32, (ROWS, ROWS), 1)
        return jnp.where(targets(h, i) == c, 1.0, 0.0).astype(BF)

    def sel_t(h, first_row, last_row):
        i = lax.broadcasted_iota(jnp.int32, (ROWS, ROWS), 1)
        c = lax.broadcasted_iota(jnp.int32, (ROWS, ROWS), 0)
        level = {0: 1, 128: 2, 192: 3}[first_row]
        n = (last_row - first_row) // 2
        j = i - first_row
        o = offs[level, 3 * par + h] & (2**level - 1)
        hit = ((j // n) * 128 + (j % n) * 2**level + o == c) & (i >= first_row) & (i < last_row)
        return jnp.where(hit, 1.0, 0.0).astype(BF)

    def role_seq(role, yy):
        return seq_at(yy, zh, (role + 2 * core) % 4)

    x_of = (x + 2 * core) % 4

    def at(ref, first_row, n):
        return ref.at[pl.ds(pl.multiple_of(first_row, n), n)]

    s2 = (y % 2) * 4 + x
    s3 = y * 4 + x
    y2 = y - y % 2

    L2_AT = ((3, 0, 1), (3, 0, 2), (3, 1, 1))
    L3_AT = ((3, 1), (3, 3), (2, 0))

    def l0_kv(blk, h):
        b = blk % 2
        return KV.at[blk, h], at(K.at[0], x * 512 + b * 256, 256), ls.at[h, b], lr.at[0], role_seq(h, y)

    def l1_kv(blk, h):
        return ZKV1.at[h, blk], at(K.at[1], x * 512 + blk * 128, 128), ls.at[3 + h, blk], lr.at[2], role_seq(h, y)

    def l2_kv(blk, h):
        role, dy, c = L2_AT[h]
        dst = at(K.at[c], s2 * 256 + blk * 64, 64)
        return ZKV2.at[h, blk], dst, ls.at[6 + h, blk], lr.at[2 * c], role_seq(role, y2 + dy)

    def l3_kv(blk, h):
        role, yy = L3_AT[h]
        return ZKV3.at[h, blk], at(K.at[2], s3 * 128 + blk * 32, 32), ls.at[9 + h, blk], lr.at[4], role_seq(role, yy)

    def near_queries(blk, h):
        b = blk % 2
        return [
            (PQ0.at[h, b], at(Q.at[x // 2], (x % 2) * 256 + b * 128, 128), ls.at[12 + h, b], lr.at[1], role_seq(h, y)),
            (PQ1.at[h, b], at(Q.at[2], x * 128 + b * 64, 64), ls.at[12 + h, 2 + b], lr.at[3], role_seq(h, y)),
        ]

    def far_queries(blk, h):
        b = blk % 2
        r2, dy, c = L2_AT[h]
        r3, yy = L3_AT[h]
        dst = at(Q.at[c + 1], s2 * 64 + b * 32, 32)
        return [
            (PQ2.at[h, b], dst, ls.at[15 + h, b], lr.at[2 * c + 1], role_seq(r2, y2 + dy)),
            (PQ3.at[h, b], at(Q.at[3], s3 * 32 + b * 16, 16), ls.at[15 + h, 2 + b], lr.at[5], role_seq(r3, yy)),
        ]

    def project_head(xs, blk, h):
        own_pair = blk // 2 == p
        yh = mm(xs, W3[h]).astype(BF)
        KV[blk, h] = yh[:, :128]

        @pl.when(own_pair)
        def _():
            PQ0[h, blk % 2] = jnp.where(low, yh[:128, 128:], yh[128:, 128:])
            send(*l0_kv(blk, h))

        z = mm(sel(h), yh).astype(BF)
        ZKV1[h, blk] = z[0:128, :128]
        ZKV2[h, blk] = z[128:192, :128]
        ZKV3[h, blk] = z[192:224, :128]
        send(*l1_kv(blk, h))

        @pl.when(own_pair)
        def _():
            b = blk % 2
            PQ1[h, b] = jnp.where(low, z[0:64, 128:], z[64:128, 128:])
            PQ2[h, b] = jnp.where(low, z[128:160, 128:], z[160:192, 128:])
            PQ3[h, b] = jnp.where(low, z[192:208, 128:], z[208:224, 128:])
            for a in near_queries(blk, h):
                send(*a)

    def project(x_ref, blk):
        xs = x_ref[...]
        for h in range(3):
            project_head(xs, blk, h)

    def far_levels(blk):
        for h in range(3):
            send(*l2_kv(blk, h))
            send(*l3_kv(blk, h))

        @pl.when(blk // 2 == p)
        def _():
            for h in range(3):
                for a in far_queries(blk, h):
                    send(*a)

    def fwd(src_slot, dst_slot, sub, part, n, dev):
        c = rcopy(T.at[src_slot, rows_of(sub, part)], T.at[dst_slot, rows_of(sub, part)], ts.at[n], tr.at[n], dev)
        c.start()
        sends.append(c)

    def share(slot, sub, n):
        r = rows_of(sub, (0, 64))
        c = rcopy(T.at[slot, r], T.at[slot, r], cs.at[n], cr.at[n], n_core)
        c.start()
        sends.append(c)

    def landed(slot, sub, part, n):
        arrived(T.at[slot, rows_of(sub, part)], tr.at[n])

    def shared(slot, sub, n):
        arrived(T.at[slot, other_rows(sub)], cr.at[n])

    for k, part in enumerate(FAR):
        landed(0, zl, part, k)
        fwd(0, 1, zl, part, 6 + k, n_in)
    share(0, zl, 0)
    pl.semaphore_wait(sxa, 2)
    tell(sya, y_next)
    project(TOK, zh)
    pl.semaphore_wait(sya, 2)
    tell(sxb, x_next)
    for k, part in enumerate(NEAR):
        landed(0, 1 - zl, part, 4 + k)
        fwd(0, 1, 1 - zl, part, 10 + k, n_in)
    share(0, 1 - zl, 1)
    for k, part in enumerate(FAR):
        landed(1, 1 - zl, part, 6 + k)
        fwd(1, 2, 1 - zl, part, 12 + k, n_out)
    share(1, 1 - zl, 2)
    pl.semaphore_wait(sxb, 2)
    far_levels(zh)
    shared(0, zl, 0)
    shared(0, 1 - zl, 1)
    for k, part in enumerate(FAR):
        if k < 3:
            project_head(T[0], g_out, k)
        landed(2, zl, part, 12 + k)
        fwd(2, 2, zl, part, 16 + k, n_in)
    share(2, zl, 4)
    far_levels(g_out)
    for k, part in enumerate(NEAR):
        landed(1, zl, part, 10 + k)
    share(1, zl, 3)
    shared(1, 1 - zl, 2)
    shared(1, zl, 3)
    project(T.at[1], (zh - dz + 4) % 4)
    far_levels((zh - dz + 4) % 4)

    def attend(t):
        job = jnp.maximum(t - 1, 0)
        VX[...] = jnp.where(low, jnp.ones((), BF), K[job])
        q = Q[t]
        qa = jnp.where(low, q, jnp.zeros((), BF))
        qb = jnp.where(low, pltpu.roll(q.astype(F32), 64, 1).astype(BF), jnp.zeros((), BF))
        k = K[job]
        v = VX[...]

        sa, sb = nt(qa, k), nt(qb, k)
        ma = jnp.max(sa, axis=1, keepdims=True)
        mb = jnp.max(sb, axis=1, keepdims=True)
        ua = mm(jnp.exp2((sa - ma) * (SCALE * LOG2E)).astype(BF), v)
        ub = mm(jnp.exp2((sb - mb) * (SCALE * LOG2E)).astype(BF), v)
        ra = pltpu.roll(ua, 64, 1)
        rb = pltpu.roll(ub, 64, 1)
        tot = jnp.where(low, ua, rb)
        o = jnp.where(low, ra, ub) / tot
        ll = SCALE * jnp.where(low, ma, mb) + jnp.log(tot)
        hi = ll.astype(BF)
        left = ll - hi.astype(F32)
        mid = left.astype(BF)
        tail = (left - mid.astype(F32)).astype(BF)
        l64 = lane & 63
        piece = jnp.where(l64 == 0, hi, jnp.where(l64 == 1, mid, jnp.where(l64 == 2, tail, jnp.zeros((), BF))))
        R[t, :, 0:128] = o.astype(BF)
        R[t, :, 128:256] = piece

    def ret0(xs):
        src = at(R.at[xs // 2], (xs % 2) * 256, 256)
        return src, R0.at[x_of], rs.at[xs], rr0.at[x_of], seq_at(y, zh, xs)

    def ret1(xs):
        return at(R.at[2], xs * 128, 128), R123.at[x_of, 0:128], rs.at[4 + xs], rr.at[x_of, 0], seq_at(y, zh, xs)

    def ret2(tile, head, first):
        def one(si):
            dst = seq_at(y2 + si // 4, zh, si % 4)
            return at(R.at[tile], si * 64, 64), R123.at[head, 128:192], rs.at[first + si], rr.at[head, 1], dst

        return one

    head_3 = jnp.where(x_of == 2, 2, y // 2)

    def ret3(si):
        dst = seq_at(si // 4, zh, si % 4)
        return at(R.at[3], si * 32, 32), R123.at[head_3, 192:224], rs.at[12 + si], rr.at[head_3, 2], dst

    ret2b = ret2(2, 2 * (y % 2), 4)
    ret2c = ret2(3, 1, 12)
    is_l2c = (x_of == 3) & (y % 2 == 0)
    is_l3 = ((x_of == 3) & (y % 2 == 1)) | ((x_of == 2) & (y == 0))

    def do_all(n, f, act):
        @pl.loop(0, n)
        def _(k):
            act(*f(k))

    for k, part in enumerate(FAR):
        landed(2, 1 - zl, part, 16 + k)
    share(2, 1 - zl, 5)
    shared(2, zl, 4)
    shared(2, 1 - zl, 5)
    project(T.at[2], (zh + 2) % 4)
    far_levels((zh + 2) % 4)

    load_wout.wait()

    def w_rows(first_row, n):
        return WF.at[pl.ds(pl.multiple_of(first_row, 64), n)]

    w_core = rcopy(WF.at[own_w], WF.at[own_w], ws.at[0], wr.at[0], n_core)
    w_in = rcopy(w_rows(384 * hd, 192), w_rows(384 * hd, 192), ws.at[1], wr.at[1], n_in)
    w_out = rcopy(w_rows(384 * hd + 192, 192), w_rows(384 * hd + 192, 192), ws.at[2], wr.at[2], n_out)
    for c in (w_core, w_in, w_out):
        c.start()
        sends.append(c)

    first = jnp.where(x_of == 3, 2, 0)
    last = jnp.where(is_l2c | is_l3, 4, 3)

    @pl.loop(first, last)
    def _(t):
        for n, first_tile in enumerate((0, 2, 3)):

            @pl.when(t == first_tile)
            def _():
                arrived(K.at[n], lr.at[2 * n])
                if n == 0:
                    arrived(Q.at[0:2], lr.at[1])
                else:
                    arrived(Q.at[n + 1], lr.at[2 * n + 1])

        attend(t)

        @pl.when(t < 2)
        def _():
            send(*ret0(2 * t))
            send(*ret0(2 * t + 1))

        @pl.when((t == 2) & (x_of != 3))
        def _():
            do_all(4, ret1, send)

        @pl.when((t == 2) & (x_of == 3))
        def _():
            do_all(8, ret2b, send)

        @pl.when((t == 3) & is_l2c)
        def _():
            do_all(8, ret2c, send)

        @pl.when((t == 3) & is_l3)
        def _():
            do_all(16, ret3, send)

    hd_in = (1 - zl) * 2 + core
    arrived(w_rows(384 * hd_in, 192), wr.at[1])
    arrived(w_rows(384 * hd_in + 192, 192), wr.at[2])
    w_pass = rcopy(w_rows(384 * hd_in, 384), w_rows(384 * hd_in, 384), ws.at[3], wr.at[3], n_core)
    w_pass.start()
    sends.append(w_pass)

    R123[:, 224:256] = jnp.zeros((3, 32, 256), BF)
    ji = lax.broadcasted_iota(jnp.int32, (128, 128), 0)
    jo = lax.broadcasted_iota(jnp.int32, (128, 128), 1)
    spread = jnp.where((ji // 64 == jo // 64) & (ji % 64 < 3), 1.0, 0.0).astype(BF)
    row = lax.broadcasted_iota(jnp.int32, (ROWS, 128), 0)
    for h in (1, 0, 2):
        arrived(R0.at[h], rr0.at[h])
        arrived(R123.at[h, 0:128], rr.at[h, 0])
        arrived(R123.at[h, 128:192], rr.at[h, 1])
        arrived(R123.at[h, 192:224], rr.at[h, 2])
        r0 = R0[h]
        os = [r0[:, :128].astype(F32)]
        logs = [mm(r0[:, 128:], spread)]
        r = R123[h]
        for l, (lo_row, hi_row) in ((1, (0, 128)), (2, (128, 192)), (3, (192, 224))):
            sc = mm(sel_t(h, lo_row, hi_row), r)
            os.append(sc[:, :128])
            lg = mm(sc[:, 128:].astype(BF), spread)
            o_l = offs[l, 3 * par + h] & (2**l - 1)
            logs.append(jnp.where((row & (2**l - 1)) == o_l, lg, ABSENT))
        best = jnp.maximum(jnp.maximum(logs[0], logs[1]), jnp.maximum(logs[2], logs[3]))
        wts = [jnp.exp(v - best) for v in logs]
        den = wts[0] + wts[1] + wts[2] + wts[3]
        num = wts[0] * os[0] + wts[1] * os[1] + wts[2] * os[2] + wts[3] * os[3]
        a = num / den
        CA[h] = a
        CR[h] = pltpu.roll(a, 64, 1)

    slot = par * 4 + hd
    for i in range(4):
        LO, HI = (CA, CR) if i < 2 else (CR, CA)
        two = jnp.where(low, LO[par], HI[par + 1])
        lo1, hi1 = LO[2 - 2 * par], HI[2 - 2 * par]
        for b in range(2):
            r = b * 128 + (i % 2) * 64
            MS[b, i, 0:64] = two[r:r + 64].astype(BF)
            MS[b, i, 64:96] = jnp.where(low, lo1[r:r + 32], hi1[r + 32:r + 64]).astype(BF)

    def final(b, i):
        return MS.at[b, i], AT.at[slot], fs.at[b * 4 + i], fr.at[slot], seq_at(y, 2 * p + b, x), i

    @pl.loop(0, 8)
    def _(n):
        src, dst, ssem, rsem, dseq, dhd = final(n // 4, n % 4)

        @pl.when((dseq != sq) | (dhd != hd))
        def _():
            rcopy(src, dst, ssem, rsem, (dseq, dhd)).start()

        @pl.when((dseq == sq) & (dhd == hd))
        def _():
            pltpu.make_async_copy(src, dst, rsem).start()

    arrived(WF.at[pl.ds(pl.multiple_of(384 * (hd + 1 - 2 * core), 128), 384)], wr.at[0])
    arrived(WF.at[pl.ds(pl.multiple_of(384 * (hd_in + 1 - 2 * core), 128), 384)], wr.at[3])

    for i in range(4):
        arrived(AT.at[i], fr.at[i])
        arrived(AT.at[4 + i], fr.at[4 + i])
        e, o = AT[i], AT[4 + i]
        x0 = e[64:96].astype(F32)
        x1 = o[64:96].astype(F32)
        AF[:, i * 384:i * 384 + 128] = e[:64]
        AF[0:32, i * 384 + 128:i * 384 + 256] = jnp.where(low, x0, pltpu.roll(x1, 64, 1)).astype(BF)
        AF[32:64, i * 384 + 128:i * 384 + 256] = jnp.where(low, pltpu.roll(x0, 64, 1), x1).astype(BF)
        AF[:, i * 384 + 256:(i + 1) * 384] = o[:64]
    out[...] = mm(AF[...], WF[...]).astype(BF)

    for c in sends:
        c.wait_send()

    @pl.loop(0, 8)
    def _(n):
        src, dst, ssem, rsem, dseq, dhd = final(n // 4, n % 4)

        @pl.when((dseq != sq) | (dhd != hd))
        def _():
            rcopy(src, dst, ssem, rsem, (dseq, dhd)).wait_send()

    for h in range(3):
        for b in range(2):
            sent(*l0_kv(2 * p + b, h))
            for a in near_queries(2 * p + b, h) + far_queries(2 * p + b, h):
                sent(*a)

    @pl.loop(0, 4)
    def _(blk):
        for h in range(3):
            sent(*l1_kv(blk, h))
            sent(*l2_kv(blk, h))
            sent(*l3_kv(blk, h))

    @pl.when(x_of != 3)
    def _():
        do_all(4, ret0, sent)
        do_all(4, ret1, sent)

    @pl.when(x_of == 3)
    def _():
        do_all(8, ret2b, sent)

    @pl.when(is_l2c)
    def _():
        do_all(8, ret2c, sent)

    @pl.when(is_l3)
    def _():
        do_all(16, ret3, sent)


def local(tokens, query_weight, key_weight, value_weight, offsets, out_weight):
    vm = lambda *s: pltpu.VMEM(s, BF)
    dma = lambda *s: pltpu.SemaphoreType.DMA(s)
    return pl.pallas_call(
        body,
        out_shape=jax.ShapeDtypeStruct((64, D), BF),
        in_specs=[pl.BlockSpec(memory_space=pl.ANY)] * 5 + [pl.BlockSpec(memory_space=pltpu.SMEM)],
        out_specs=pl.BlockSpec(memory_space=pltpu.VMEM),
        scratch_shapes=[
            vm(256, D), vm(3, D, 256), vm(3, D, 256), vm(D, D),
            vm(3, 256, D), vm(4, 3, 256, 128),
            vm(3, 4, 128, 128), vm(3, 4, 64, 128), vm(3, 4, 32, 128),
            vm(3, 2, 128, 128), vm(3, 2, 64, 128), vm(3, 2, 32, 128), vm(3, 2, 16, 128),
            vm(3, 2048, 128), vm(4, 512, 128), vm(2048, 128), vm(4, 512, 256), vm(3, 256, 256), vm(3, 256, 256),
            pltpu.VMEM((3, 256, 128), F32), pltpu.VMEM((3, 256, 128), F32),
            vm(2, 4, 96, 128), vm(8, 96, 128), vm(64, D),
            dma(5), dma(20), dma(20), dma(6), dma(6), dma(18, 4), dma(6), dma(28), dma(3), dma(3, 3),
            dma(4), dma(4), dma(8), dma(8),
            pltpu.SemaphoreType.REGULAR, pltpu.SemaphoreType.REGULAR, pltpu.SemaphoreType.REGULAR,
        ],
        compiler_params=pltpu.CompilerParams(
            has_side_effects=True, collective_id=1, vmem_limit_bytes=62 * 1024 * 1024
        ),
    )(tokens, query_weight, key_weight, value_weight, out_weight, offsets)


def solution(mesh):
    return jax.shard_map(
        local,
        mesh=mesh,
        in_specs=(
            P("seq", None),
            P(None, "head"),
            P(None, "head"),
            P(None, "head"),
            P(None, "head"),
            P("head", None),
        ),
        out_specs=P(("seq", "head"), None),
        check_vma=False,
    )
```

```python
import jax
import jax.numpy as jnp
from jax import lax
from jax.experimental import pallas as pl
from jax.experimental.pallas import tpu as pltpu
from jax.sharding import PartitionSpec as P

MESH = pl.DeviceIdType.MESH
BF = jnp.bfloat16
F32 = jnp.float32
ROWS = 256
D = 1536
HALF = 128
SCALE = 0.125
LOG2E = 1.4426950408889634
ABSENT = -1e30


def nt(a, b):
    return lax.dot_general(a, b, (((1,), (1,)), ((), ())), preferred_element_type=F32)


def mm(a, b):
    return jnp.dot(a, b, preferred_element_type=F32)


def body(
    tok, wq, wk, wv, wout, offs, out,
    TOK, WIN, W3, WF, T, KV, ZKV1, ZKV2, ZKV3, PQ0, PQ1, PQ2, PQ3,
    K, Q, VX, R, R0, R123, CA, CR, MS, AT, AF,
    win, ts, tr, cs, cr, ls, lr, rs, rr0, rr, ws, wr, fs, fr,
    sxa, sya, sxb,
):
    sq = lax.axis_index("seq")
    hd = lax.axis_index("head")
    y = sq // 16
    zh = (sq // 4) % 4
    x = sq % 4
    zl = hd // 2
    core = hd % 2
    par = zh % 2
    p = zh // 2

    def seq_at(yy, zz, xx):
        return yy * 16 + zz * 4 + xx

    dz = 2 * zl - 1
    g_out = (zh + dz + 4) % 4
    n_out = (seq_at(y, g_out, x), (1 - zl) * 2 + core)
    n_in = (sq, (1 - zl) * 2 + core)
    n_core = (sq, zl * 2 + (1 - core))

    barrier = pltpu.get_barrier_semaphore()

    def hello(dev):
        pl.semaphore_signal(barrier, inc=1, device_id=dev, device_id_type=MESH)

    hello(n_out)
    hello(n_in)
    hello(n_core)
    x_next = [(seq_at(y, zh, (x + d) % 4), hd) for d in (1, 3)]
    y_next = [(seq_at((y + d) % 4, zh, x), hd) for d in (1, 3)]
    for dev in x_next + y_next:
        hello(dev)

    def tell(sem, devs):
        for dev in devs:
            pl.semaphore_signal(sem, inc=1, device_id=dev, device_id_type=MESH)

    start = pl.multiple_of(128 * par, 128)
    loads = [pltpu.make_async_copy(wsrc.at[:, pl.ds(start, 256)], WIN.at[n], win.at[n]) for n, wsrc in enumerate((wk, wv, wq))]
    own_w = pl.ds(pl.multiple_of(384 * hd, 128), 384)
    load_tok = pltpu.make_async_copy(tok, TOK, win.at[3])
    load_wout = pltpu.make_async_copy(wout, WF.at[own_w], win.at[4])
    for c in loads:
        c.start()
    load_tok.start()

    def rcopy(src, dst, ssem, rsem, dev):
        return pltpu.make_async_remote_copy(
            src_ref=src, dst_ref=dst, send_sem=ssem, recv_sem=rsem, device_id=dev, device_id_type=MESH
        )

    def send(src, dst, ssem, rsem, dst_seq):
        @pl.when(dst_seq != sq)
        def _():
            rcopy(src, dst, ssem, rsem, (dst_seq, hd)).start()

        @pl.when(dst_seq == sq)
        def _():
            pltpu.make_async_copy(src, dst, rsem).start()

    def sent(src, dst, ssem, rsem, dst_seq):
        @pl.when(dst_seq != sq)
        def _():
            rcopy(src, dst, ssem, rsem, (dst_seq, hd)).wait_send()

    def arrived(ref, sem):
        pltpu.make_async_copy(ref, ref, sem).wait()

    lane = lax.broadcasted_iota(jnp.int32, (1, 128), 1)
    low = lane < 64

    lo = core * HALF

    FAR = [(i * 16, 16) for i in range(4)]
    NEAR = [(i * 32, 32) for i in range(2)]

    def rows_of(sub, part):
        return pl.ds(pl.multiple_of(lo + sub * 64 + part[0], part[1]), part[1])

    def other_rows(sub):
        return pl.ds(pl.multiple_of(HALF - lo + sub * 64, 64), 64)

    pl.semaphore_wait(barrier, 7)
    sends = []

    def own(sub, part, n):
        c = rcopy(tok.at[rows_of(sub, part)], T.at[0, rows_of(sub, part)], ts.at[n], tr.at[n], n_out)
        c.start()
        sends.append(c)

    for k, part in enumerate(FAR):
        own(1 - zl, part, k)
    for k, part in enumerate(NEAR):
        own(zl, part, 4 + k)

    tell(sxa, x_next)

    for c in loads:
        c.wait()
    load_tok.wait()

    def mover(rows, with_part):
        r = lax.broadcasted_iota(jnp.int32, (rows, 384), 0)
        c = lax.broadcasted_iota(jnp.int32, (rows, 384), 1)
        src = 64 * par + (c // 128) * 64 + c % 64
        if with_part:
            src = src + ((c // 64) % 2) * 256
        return jnp.where(r == src, 1.0, 0.0).astype(BF)

    pkv = mover(512, True)
    pq = mover(256, False)

    @pl.loop(0, 6)
    def _(i):
        r = pl.ds(pl.multiple_of(i * 256, 256), 256)
        wkv = mm(WIN[0, r], pkv[:256]) + mm(WIN[1, r], pkv[256:])
        wqq = mm(WIN[2, r], pq)
        for h in range(3):
            W3[h, r, 0:128] = wkv[:, h * 128:(h + 1) * 128].astype(BF)
            W3[h, r, 128:256] = wqq[:, h * 128:(h + 1) * 128].astype(BF)

    load_wout.start()

    def targets(h, i):
        o1 = offs[1, 3 * par + h] & 1
        o2 = offs[2, 3 * par + h] & 3
        o3 = offs[3, 3 * par + h] & 7
        t1 = i * 2 + o1
        t2 = (i - 128) * 4 + o2
        t3 = (i - 192) * 8 + o3
        return jnp.where(i < 128, t1, jnp.where(i < 192, t2, jnp.where(i < 224, t3, -1)))

    def sel(h):
        i = lax.broadcasted_iota(jnp.int32, (ROWS, ROWS), 0)
        c = lax.broadcasted_iota(jnp.int32, (ROWS, ROWS), 1)
        return jnp.where(targets(h, i) == c, 1.0, 0.0).astype(BF)

    def sel_t(h, first_row, last_row):
        i = lax.broadcasted_iota(jnp.int32, (ROWS, ROWS), 1)
        c = lax.broadcasted_iota(jnp.int32, (ROWS, ROWS), 0)
        level = {0: 1, 128: 2, 192: 3}[first_row]
        n = (last_row - first_row) // 2
        j = i - first_row
        o = offs[level, 3 * par + h] & (2**level - 1)
        hit = ((j // n) * 128 + (j % n) * 2**level + o == c) & (i >= first_row) & (i < last_row)
        return jnp.where(hit, 1.0, 0.0).astype(BF)

    def role_seq(role, yy):
        return seq_at(yy, zh, (role + 2 * core) % 4)

    x_of = (x + 2 * core) % 4

    def at(ref, first_row, n):
        return ref.at[pl.ds(pl.multiple_of(first_row, n), n)]

    s2 = (y % 2) * 4 + x
    s3 = y * 4 + x
    y2 = y - y % 2

    L2_AT = ((3, 0, 1), (3, 0, 2), (3, 1, 1))
    L3_AT = ((3, 1), (3, 3), (2, 0))

    def l0_kv(blk, h):
        b = blk % 2
        return KV.at[blk, h], at(K.at[0], x * 512 + b * 256, 256), ls.at[h, b], lr.at[0], role_seq(h, y)

    def l1_kv(blk, h):
        return ZKV1.at[h, blk], at(K.at[1], x * 512 + blk * 128, 128), ls.at[3 + h, blk], lr.at[2], role_seq(h, y)

    def l2_kv(blk, h):
        role, dy, c = L2_AT[h]
        dst = at(K.at[c], s2 * 256 + blk * 64, 64)
        return ZKV2.at[h, blk], dst, ls.at[6 + h, blk], lr.at[2 * c], role_seq(role, y2 + dy)

    def l3_kv(blk, h):
        role, yy = L3_AT[h]
        return ZKV3.at[h, blk], at(K.at[2], s3 * 128 + blk * 32, 32), ls.at[9 + h, blk], lr.at[4], role_seq(role, yy)

    def near_queries(blk, h):
        b = blk % 2
        return [
            (PQ0.at[h, b], at(Q.at[x // 2], (x % 2) * 256 + b * 128, 128), ls.at[12 + h, b], lr.at[1], role_seq(h, y)),
            (PQ1.at[h, b], at(Q.at[2], x * 128 + b * 64, 64), ls.at[12 + h, 2 + b], lr.at[3], role_seq(h, y)),
        ]

    def far_queries(blk, h):
        b = blk % 2
        r2, dy, c = L2_AT[h]
        r3, yy = L3_AT[h]
        dst = at(Q.at[c + 1], s2 * 64 + b * 32, 32)
        return [
            (PQ2.at[h, b], dst, ls.at[15 + h, b], lr.at[2 * c + 1], role_seq(r2, y2 + dy)),
            (PQ3.at[h, b], at(Q.at[3], s3 * 32 + b * 16, 16), ls.at[15 + h, 2 + b], lr.at[5], role_seq(r3, yy)),
        ]

    def project_head(xs, blk, h):
        own_pair = blk // 2 == p
        yh = mm(xs, W3[h]).astype(BF)
        KV[blk, h] = yh[:, :128]

        @pl.when(own_pair)
        def _():
            PQ0[h, blk % 2] = jnp.where(low, yh[:128, 128:], yh[128:, 128:])
            send(*l0_kv(blk, h))

        z = mm(sel(h), yh).astype(BF)
        ZKV1[h, blk] = z[0:128, :128]
        ZKV2[h, blk] = z[128:192, :128]
        ZKV3[h, blk] = z[192:224, :128]
        send(*l1_kv(blk, h))

        @pl.when(own_pair)
        def _():
            b = blk % 2
            PQ1[h, b] = jnp.where(low, z[0:64, 128:], z[64:128, 128:])
            PQ2[h, b] = jnp.where(low, z[128:160, 128:], z[160:192, 128:])
            PQ3[h, b] = jnp.where(low, z[192:208, 128:], z[208:224, 128:])
            for a in near_queries(blk, h):
                send(*a)

    def project(x_ref, blk):
        xs = x_ref[...]
        for h in range(3):
            project_head(xs, blk, h)

    def far_levels(blk):
        for h in range(3):
            send(*l2_kv(blk, h))
            send(*l3_kv(blk, h))

        @pl.when(blk // 2 == p)
        def _():
            for h in range(3):
                for a in far_queries(blk, h):
                    send(*a)

    def fwd(src_slot, dst_slot, sub, part, n, dev):
        c = rcopy(T.at[src_slot, rows_of(sub, part)], T.at[dst_slot, rows_of(sub, part)], ts.at[n], tr.at[n], dev)
        c.start()
        sends.append(c)

    def share(slot, sub, n):
        r = rows_of(sub, (0, 64))
        c = rcopy(T.at[slot, r], T.at[slot, r], cs.at[n], cr.at[n], n_core)
        c.start()
        sends.append(c)

    def landed(slot, sub, part, n):
        arrived(T.at[slot, rows_of(sub, part)], tr.at[n])

    def shared(slot, sub, n):
        arrived(T.at[slot, other_rows(sub)], cr.at[n])

    for k, part in enumerate(FAR):
        landed(0, zl, part, k)
        fwd(0, 1, zl, part, 6 + k, n_in)
    share(0, zl, 0)
    pl.semaphore_wait(sxa, 2)
    tell(sya, y_next)
    project(TOK, zh)
    pl.semaphore_wait(sya, 2)
    tell(sxb, x_next)
    for k, part in enumerate(NEAR):
        landed(0, 1 - zl, part, 4 + k)
        fwd(0, 1, 1 - zl, part, 10 + k, n_in)
    share(0, 1 - zl, 1)
    for k, part in enumerate(FAR):
        landed(1, 1 - zl, part, 6 + k)
        fwd(1, 2, 1 - zl, part, 12 + k, n_out)
    share(1, 1 - zl, 2)
    pl.semaphore_wait(sxb, 2)
    far_levels(zh)
    shared(0, zl, 0)
    shared(0, 1 - zl, 1)
    for k, part in enumerate(FAR):
        if k < 3:
            project_head(T[0], g_out, k)
        landed(2, zl, part, 12 + k)
        fwd(2, 2, zl, part, 16 + k, n_in)
    share(2, zl, 4)
    far_levels(g_out)
    for k, part in enumerate(NEAR):
        landed(1, zl, part, 10 + k)
    share(1, zl, 3)
    shared(1, 1 - zl, 2)
    shared(1, zl, 3)
    project(T.at[1], (zh - dz + 4) % 4)
    far_levels((zh - dz + 4) % 4)

    def attend(t):
        job = jnp.maximum(t - 1, 0)
        VX[...] = jnp.where(low, jnp.ones((), BF), K[job])
        q = Q[t]
        qa = jnp.where(low, q, jnp.zeros((), BF))
        qb = jnp.where(low, pltpu.roll(q.astype(F32), 64, 1).astype(BF), jnp.zeros((), BF))
        k = K[job]
        v = VX[...]

        sa, sb = nt(qa, k), nt(qb, k)
        ma = jnp.max(sa, axis=1, keepdims=True)
        mb = jnp.max(sb, axis=1, keepdims=True)
        ua = mm(jnp.exp2((sa - ma) * (SCALE * LOG2E)).astype(BF), v)
        ub = mm(jnp.exp2((sb - mb) * (SCALE * LOG2E)).astype(BF), v)
        ra = pltpu.roll(ua, 64, 1)
        rb = pltpu.roll(ub, 64, 1)
        tot = jnp.where(low, ua, rb)
        o = jnp.where(low, ra, ub) / tot
        ll = SCALE * jnp.where(low, ma, mb) + jnp.log(tot)
        hi = ll.astype(BF)
        left = ll - hi.astype(F32)
        mid = left.astype(BF)
        tail = (left - mid.astype(F32)).astype(BF)
        l64 = lane & 63
        piece = jnp.where(l64 == 0, hi, jnp.where(l64 == 1, mid, jnp.where(l64 == 2, tail, jnp.zeros((), BF))))
        R[t, :, 0:128] = o.astype(BF)
        R[t, :, 128:256] = piece

    def ret0(xs):
        src = at(R.at[xs // 2], (xs % 2) * 256, 256)
        return src, R0.at[x_of], rs.at[xs], rr0.at[x_of], seq_at(y, zh, xs)

    def ret1(xs):
        return at(R.at[2], xs * 128, 128), R123.at[x_of, 0:128], rs.at[4 + xs], rr.at[x_of, 0], seq_at(y, zh, xs)

    def ret2(tile, head, first):
        def one(si):
            dst = seq_at(y2 + si // 4, zh, si % 4)
            return at(R.at[tile], si * 64, 64), R123.at[head, 128:192], rs.at[first + si], rr.at[head, 1], dst

        return one

    head_3 = jnp.where(x_of == 2, 2, y // 2)

    def ret3(si):
        dst = seq_at(si // 4, zh, si % 4)
        return at(R.at[3], si * 32, 32), R123.at[head_3, 192:224], rs.at[12 + si], rr.at[head_3, 2], dst

    ret2b = ret2(2, 2 * (y % 2), 4)
    ret2c = ret2(3, 1, 12)
    is_l2c = (x_of == 3) & (y % 2 == 0)
    is_l3 = ((x_of == 3) & (y % 2 == 1)) | ((x_of == 2) & (y == 0))

    def do_all(n, f, act):
        @pl.loop(0, n)
        def _(k):
            act(*f(k))

    for k, part in enumerate(FAR):
        landed(2, 1 - zl, part, 16 + k)
    share(2, 1 - zl, 5)
    shared(2, zl, 4)
    shared(2, 1 - zl, 5)
    far_blk = (zh + 2) % 4
    xs_far = T[2]
    for h in range(3):
        z = mm(sel(h), mm(xs_far, W3[h, :, 0:128]).astype(BF)).astype(BF)
        ZKV1[h, far_blk] = z[0:128]
        ZKV2[h, far_blk] = z[128:192]
        ZKV3[h, far_blk] = z[192:224]
        send(*l1_kv(far_blk, h))
    far_levels((zh + 2) % 4)

    load_wout.wait()

    def w_rows(first_row, n):
        return WF.at[pl.ds(pl.multiple_of(first_row, 64), n)]

    w_core = rcopy(WF.at[own_w], WF.at[own_w], ws.at[0], wr.at[0], n_core)
    w_in = rcopy(w_rows(384 * hd, 192), w_rows(384 * hd, 192), ws.at[1], wr.at[1], n_in)
    w_out = rcopy(w_rows(384 * hd + 192, 192), w_rows(384 * hd + 192, 192), ws.at[2], wr.at[2], n_out)
    for c in (w_core, w_in, w_out):
        c.start()
        sends.append(c)

    first = jnp.where(x_of == 3, 2, 0)
    last = jnp.where(is_l2c | is_l3, 4, 3)

    @pl.loop(first, last)
    def _(t):
        for n, first_tile in enumerate((0, 2, 3)):

            @pl.when(t == first_tile)
            def _():
                arrived(K.at[n], lr.at[2 * n])
                if n == 0:
                    arrived(Q.at[0:2], lr.at[1])
                else:
                    arrived(Q.at[n + 1], lr.at[2 * n + 1])

        attend(t)

        @pl.when(t < 2)
        def _():
            send(*ret0(2 * t))
            send(*ret0(2 * t + 1))

        @pl.when((t == 2) & (x_of != 3))
        def _():
            do_all(4, ret1, send)

        @pl.when((t == 2) & (x_of == 3))
        def _():
            do_all(8, ret2b, send)

        @pl.when((t == 3) & is_l2c)
        def _():
            do_all(8, ret2c, send)

        @pl.when((t == 3) & is_l3)
        def _():
            do_all(16, ret3, send)

    hd_in = (1 - zl) * 2 + core
    arrived(w_rows(384 * hd_in, 192), wr.at[1])
    arrived(w_rows(384 * hd_in + 192, 192), wr.at[2])
    w_pass = rcopy(w_rows(384 * hd_in, 384), w_rows(384 * hd_in, 384), ws.at[3], wr.at[3], n_core)
    w_pass.start()
    sends.append(w_pass)

    R123[:, 224:256] = jnp.zeros((3, 32, 256), BF)
    ji = lax.broadcasted_iota(jnp.int32, (128, 128), 0)
    jo = lax.broadcasted_iota(jnp.int32, (128, 128), 1)
    spread = jnp.where((ji // 64 == jo // 64) & (ji % 64 < 3), 1.0, 0.0).astype(BF)
    row = lax.broadcasted_iota(jnp.int32, (ROWS, 128), 0)
    for h in (1, 0, 2):
        arrived(R0.at[h], rr0.at[h])
        arrived(R123.at[h, 0:128], rr.at[h, 0])
        arrived(R123.at[h, 128:192], rr.at[h, 1])
        arrived(R123.at[h, 192:224], rr.at[h, 2])
        r0 = R0[h]
        os = [r0[:, :128].astype(F32)]
        logs = [mm(r0[:, 128:], spread)]
        r = R123[h]
        for l, (lo_row, hi_row) in ((1, (0, 128)), (2, (128, 192)), (3, (192, 224))):
            sc = mm(sel_t(h, lo_row, hi_row), r)
            os.append(sc[:, :128])
            lg = mm(sc[:, 128:].astype(BF), spread)
            o_l = offs[l, 3 * par + h] & (2**l - 1)
            logs.append(jnp.where((row & (2**l - 1)) == o_l, lg, ABSENT))
        best = jnp.maximum(jnp.maximum(logs[0], logs[1]), jnp.maximum(logs[2], logs[3]))
        wts = [jnp.exp(v - best) for v in logs]
        den = wts[0] + wts[1] + wts[2] + wts[3]
        num = wts[0] * os[0] + wts[1] * os[1] + wts[2] * os[2] + wts[3] * os[3]
        a = num / den
        CA[h] = a
        CR[h] = pltpu.roll(a, 64, 1)

    slot = par * 4 + hd
    for i in range(4):
        LO, HI = (CA, CR) if i < 2 else (CR, CA)
        two = jnp.where(low, LO[par], HI[par + 1])
        lo1, hi1 = LO[2 - 2 * par], HI[2 - 2 * par]
        for b in range(2):
            r = b * 128 + (i % 2) * 64
            MS[b, i, 0:64] = two[r:r + 64].astype(BF)
            MS[b, i, 64:96] = jnp.where(low, lo1[r:r + 32], hi1[r + 32:r + 64]).astype(BF)

    def final(b, i):
        return MS.at[b, i], AT.at[slot], fs.at[b * 4 + i], fr.at[slot], seq_at(y, 2 * p + b, x), i

    @pl.loop(0, 8)
    def _(n):
        src, dst, ssem, rsem, dseq, dhd = final(n // 4, n % 4)

        @pl.when((dseq != sq) | (dhd != hd))
        def _():
            rcopy(src, dst, ssem, rsem, (dseq, dhd)).start()

        @pl.when((dseq == sq) & (dhd == hd))
        def _():
            pltpu.make_async_copy(src, dst, rsem).start()

    arrived(WF.at[pl.ds(pl.multiple_of(384 * (hd + 1 - 2 * core), 128), 384)], wr.at[0])
    arrived(WF.at[pl.ds(pl.multiple_of(384 * (hd_in + 1 - 2 * core), 128), 384)], wr.at[3])

    for i in range(4):
        arrived(AT.at[i], fr.at[i])
        arrived(AT.at[4 + i], fr.at[4 + i])
        e, o = AT[i], AT[4 + i]
        x0 = e[64:96].astype(F32)
        x1 = o[64:96].astype(F32)
        AF[:, i * 384:i * 384 + 128] = e[:64]
        AF[0:32, i * 384 + 128:i * 384 + 256] = jnp.where(low, x0, pltpu.roll(x1, 64, 1)).astype(BF)
        AF[32:64, i * 384 + 128:i * 384 + 256] = jnp.where(low, pltpu.roll(x0, 64, 1), x1).astype(BF)
        AF[:, i * 384 + 256:(i + 1) * 384] = o[:64]
    out[...] = mm(AF[...], WF[...]).astype(BF)

    for c in sends:
        c.wait_send()

    @pl.loop(0, 8)
    def _(n):
        src, dst, ssem, rsem, dseq, dhd = final(n // 4, n % 4)

        @pl.when((dseq != sq) | (dhd != hd))
        def _():
            rcopy(src, dst, ssem, rsem, (dseq, dhd)).wait_send()

    for h in range(3):
        for b in range(2):
            sent(*l0_kv(2 * p + b, h))
            for a in near_queries(2 * p + b, h) + far_queries(2 * p + b, h):
                sent(*a)

    @pl.loop(0, 4)
    def _(blk):
        for h in range(3):
            sent(*l1_kv(blk, h))
            sent(*l2_kv(blk, h))
            sent(*l3_kv(blk, h))

    @pl.when(x_of != 3)
    def _():
        do_all(4, ret0, sent)
        do_all(4, ret1, sent)

    @pl.when(x_of == 3)
    def _():
        do_all(8, ret2b, sent)

    @pl.when(is_l2c)
    def _():
        do_all(8, ret2c, sent)

    @pl.when(is_l3)
    def _():
        do_all(16, ret3, sent)


def local(tokens, query_weight, key_weight, value_weight, offsets, out_weight):
    vm = lambda *s: pltpu.VMEM(s, BF)
    dma = lambda *s: pltpu.SemaphoreType.DMA(s)
    return pl.pallas_call(
        body,
        out_shape=jax.ShapeDtypeStruct((64, D), BF),
        in_specs=[pl.BlockSpec(memory_space=pl.ANY)] * 5 + [pl.BlockSpec(memory_space=pltpu.SMEM)],
        out_specs=pl.BlockSpec(memory_space=pltpu.VMEM),
        scratch_shapes=[
            vm(256, D), vm(3, D, 256), vm(3, D, 256), vm(D, D),
            vm(3, 256, D), vm(4, 3, 256, 128),
            vm(3, 4, 128, 128), vm(3, 4, 64, 128), vm(3, 4, 32, 128),
            vm(3, 2, 128, 128), vm(3, 2, 64, 128), vm(3, 2, 32, 128), vm(3, 2, 16, 128),
            vm(3, 2048, 128), vm(4, 512, 128), vm(2048, 128), vm(4, 512, 256), vm(3, 256, 256), vm(3, 256, 256),
            pltpu.VMEM((3, 256, 128), F32), pltpu.VMEM((3, 256, 128), F32),
            vm(2, 4, 96, 128), vm(8, 96, 128), vm(64, D),
            dma(5), dma(20), dma(20), dma(6), dma(6), dma(18, 4), dma(6), dma(28), dma(3), dma(3, 3),
            dma(4), dma(4), dma(8), dma(8),
            pltpu.SemaphoreType.REGULAR, pltpu.SemaphoreType.REGULAR, pltpu.SemaphoreType.REGULAR,
        ],
        compiler_params=pltpu.CompilerParams(
            has_side_effects=True, collective_id=1, vmem_limit_bytes=62 * 1024 * 1024
        ),
    )(tokens, query_weight, key_weight, value_weight, out_weight, offsets)


def solution(mesh):
    return jax.shard_map(
        local,
        mesh=mesh,
        in_specs=(
            P("seq", None),
            P(None, "head"),
            P(None, "head"),
            P(None, "head"),
            P(None, "head"),
            P("head", None),
        ),
        out_specs=P(("seq", "head"), None),
        check_vma=False,
    )
```
